512 devices in a mesh: il: 8 (over z_lo), xl: 8 (over y, core), gz: 8 (over z_hi, x).
Axes of the slice: x: 4, y: 4, z: 16 (z_hi: 2, z_lo: 8; z = z_hi * 8 + z_lo), core: 2. Of those that a mesh axis runs over, the one named last changes fastest.
Arguments:
- reflect: float32 [320, 320, 1024], P('il', 'xl', 'gz'), may hold values from -6 to 6
- weights: bfloat16 [2, 320, 320, 1024], P(None, 'il', 'xl', 'gz'), may hold values from 0.099609375 to 1
- cell_slot: int32 [2, 320, 320, 1024], P(None, 'il', 'xl', 'gz'), may hold values from 0 to 2, as said below
- factors: bfloat16 [2048, 1536], P(('il', 'xl', 'gz')), may hold values from -0.5390625 to 0.5390625
- reader_list: int32 [8, 8, 8, 3], P('il', 'xl', 'gz'), may hold values from -1 to 2047, as said below
Outputs:
- image: float32 [320, 320, 1024], P('il', 'xl', 'gz')
The draws below stay inside these ranges and needn't reach their ends.
Inputs may be any that keep to these rules, and one draw needn't show every extreme that they name: `reader_list`: row g of factors belongs to the device at position g // 4 of the devices in order il, xl, gz. A device's list holds 1 to 3 distinct ids first and -1 after them; 3 on some device. Every id belongs to a device with the same il and gz index, and at most 2 ids of a list to one device, 2 reached on some device. `cell_slot`: each entry points into the first part of its device's list, which holds ids.
All inputs are finite; a program needn't handle non-finite values.
Results may differ from the reference program's by a relative error of at most 0.005.
Values may be sent and summed in bfloat16 or wider, within the bound.
No kernel may reach another device: no remote copies, remote signals or barrier semaphores. Data moves between devices by JAX's collectives and lax.ppermute only.
A program may use at most 64 MiB of HBM per device.

```python
import jax
import jax.numpy as jnp
import numpy as np
from jax import lax

K = 64
R = 8
J = 2
CP_DEV = 4
NEED = 3
SLOTS = 2
CX = 40
CY = 40
CZ = 128
NX = 320
NY = 320
NZ = 1024
NCP = 2048
N_IL = 8
N_XL = 8
N_GZ = 8


def list_plan(key):
    first_key, second_key, third_key, fourth_key = jax.random.split(jax.random.fold_in(key, 11), 4)
    device_count = N_IL * N_XL * N_GZ
    random_levels = jax.random.randint(first_key, (device_count,), 0, 8)
    counts = 1 + random_levels * random_levels * (NEED - 1) // 49
    counts = counts.at[0].set(NEED)
    paired = jax.random.randint(second_key, (device_count,), 0, 2)
    paired = paired.at[0].set(1)
    shuffled = jax.vmap(lambda one_key: jax.random.permutation(one_key, N_XL))(jax.random.split(third_key, device_count))
    offsets = jax.random.randint(fourth_key, (device_count, N_XL), 0, CP_DEV)
    position = jnp.arange(NEED, dtype=jnp.int32)[None, :]
    owner_slot = jnp.where(paired[:, None] == 1, position // SLOTS, position)
    slot_index = jnp.where(paired[:, None] == 1, position % SLOTS, 0)
    owner_index = jnp.take_along_axis(shuffled, owner_slot, axis=1)
    local_row = (jnp.take_along_axis(offsets, owner_index, axis=1) + slot_index) % CP_DEV
    device_ids = jnp.arange(device_count, dtype=jnp.int32)[:, None]
    inline_index = device_ids // (N_XL * N_GZ)
    depth_index = device_ids % N_GZ
    global_id = ((inline_index * N_XL + owner_index) * N_GZ + depth_index) * CP_DEV + local_row
    listing = jnp.where(position < counts[:, None], global_id, -1).astype(jnp.int32)
    return (counts.astype(jnp.int32), listing.reshape(N_IL, N_XL, N_GZ, NEED))


def draw_reader_list(key, part):
    counts, listing = list_plan(key)
    return listing


def draw_cell_slot(key, part):
    counts, listing = list_plan(key)
    random_draws = jax.random.randint(jax.random.fold_in(key, 13), (J, N_IL, CX, N_XL, CY, N_GZ, CZ), 0, 1 << 20)
    grid_counts = counts.reshape(N_IL, N_XL, N_GZ)[None, :, None, :, None, :, None]
    return (random_draws % grid_counts).astype(jnp.int32).reshape(J, NX, NY, NZ)


def block_levels(rng, shape, cuts, smallest, top_value):
    level = 1.0
    for dim, blocks in cuts:
        draws = jax.random.uniform(jax.random.fold_in(jax.random.fold_in(rng, 6), dim), (blocks,), jnp.float32, smallest / len(cuts), top_value / len(cuts))
        level = level * jnp.repeat(jnp.exp(draws), shape[dim] // blocks).reshape((-1,) + (1,) * (len(shape) - 1 - dim))
    return level


def gaussian(key, dims, spread, most, cuts=(), held_as=jnp.bfloat16):
    array = spread * jax.random.normal(key, dims, jnp.float32)
    if cuts:
        array = array * block_levels(key, dims, cuts, -0.22, 0.18)
    return jnp.clip(array, -most, most).astype(held_as)


def setup_inputs(seed: int = 0) -> dict:
    key_list = jax.random.split(jax.random.key(seed), 6)
    return {
        "reflect": gaussian(key_list[0], (NX, NY, NZ), 1.0, 6.0, ((0, 8), (1, 8), (2, 8)), jnp.float32),
        "weights": jnp.clip(0.099609375 + 0.9003906 * jax.random.uniform(key_list[1], (J, NX, NY, NZ), jnp.float32) ** block_levels(key_list[1], (J, NX, NY, NZ), ((1, 8), (2, 8), (3, 8)), -0.2, 0.2), 0.099609375, 1.0).astype(jnp.bfloat16),
        "cell_slot": draw_cell_slot(jax.random.fold_in(key_list[5], 71), 0),
        "factors": gaussian(key_list[3], (NCP, 3 * R * K), 0.09, 0.5390625, ((0, 512),)),
        "reader_list": draw_reader_list(jax.random.fold_in(key_list[5], 71), 0),
    }


def banded(filters, length):
    tap_count = filters.shape[-1]
    offset = np.arange(length + tap_count)[None, :] - np.arange(length)[:, None]
    inside = (offset >= 0) & (offset < tap_count)
    picked = filters[..., np.clip(offset, 0, tap_count - 1)]
    return jnp.where(inside, picked, jnp.zeros_like(picked))


def blur_slot(extended_wide, factor_panel):
    filters = factor_panel.astype(jnp.float32).reshape(R, 3, K)
    highest = lax.Precision.HIGHEST
    summed = jnp.zeros((CX, CY, CZ), jnp.float32)
    for rank_group in range(R // 4):
        chosen = filters[4 * rank_group:4 * rank_group + 4]
        line_x = jnp.einsum("roi,iyz->royz", banded(chosen[:, 0], CX), extended_wide, precision=highest)
        line_x = lax.optimization_barrier(line_x.astype(jnp.bfloat16)).astype(jnp.float32)
        line_y = jnp.einsum("roi,rxiz->rxoz", banded(chosen[:, 1], CY), line_x, precision=highest)
        line_y = lax.optimization_barrier(line_y.astype(jnp.bfloat16)).astype(jnp.float32)
        summed = summed + jnp.einsum("roi,rxyi->xyo", banded(chosen[:, 2], CZ), line_y, precision=highest)
    return summed


def reference(reflect, weights, cell_slot, factors, reader_list):
    half_width = K // 2
    padded = jnp.pad(reflect.astype(jnp.bfloat16), half_width)
    zero_index = jnp.zeros((), jnp.int32)

    def tile_image(tile_index):
        tile_x = (tile_index // (N_XL * N_GZ)).astype(jnp.int32)
        tile_y = ((tile_index // N_GZ) % N_XL).astype(jnp.int32)
        tile_z = (tile_index % N_GZ).astype(jnp.int32)
        extended_wide = lax.dynamic_slice(padded, (tile_x * CX, tile_y * CY, tile_z * CZ), (CX + K, CY + K, CZ + K)).astype(jnp.float32)
        tile_weights = lax.dynamic_slice(weights, (zero_index, tile_x * CX, tile_y * CY, tile_z * CZ), (J, CX, CY, CZ)).astype(jnp.float32)
        tile_slots = lax.dynamic_slice(cell_slot, (zero_index, tile_x * CX, tile_y * CY, tile_z * CZ), (J, CX, CY, CZ))
        listed = lax.dynamic_slice(reader_list, (tile_x, tile_y, tile_z, zero_index), (1, 1, 1, NEED)).reshape(NEED)
        live_count = jnp.sum((listed >= 0).astype(jnp.int32)).astype(jnp.int32)

        def add_slot(slot_index, blurred_sum):
            global_id = jnp.maximum(listed[slot_index], 0).astype(jnp.int32)
            factor_panel = lax.dynamic_index_in_dim(factors, global_id, 0, keepdims=False)
            weight_map = jnp.sum(jnp.where(tile_slots == slot_index, tile_weights, jnp.zeros_like(tile_weights)), axis=0)
            return blurred_sum + weight_map * blur_slot(extended_wide, factor_panel)

        return lax.fori_loop(jnp.zeros((), jnp.int32), live_count, add_slot, jnp.zeros((CX, CY, CZ), jnp.float32))

    tiles = lax.map(tile_image, jnp.arange(N_IL * N_XL * N_GZ, dtype=jnp.int32))
    tiles = tiles.reshape(N_IL, N_XL, N_GZ, CX, CY, CZ).transpose(0, 3, 1, 4, 2, 5)
    return tiles.reshape(NX, NY, NZ)
```

```python
import jax
import jax.numpy as jnp
import numpy as np
from jax import lax
from jax.sharding import PartitionSpec as P

K = 64
R = 8
CP_DEV = 4
NEED = 3


def padded(cells, sides, width):
    for axis, dim in sides:
        count = lax.axis_size(axis)
        ends = count - 1
        head = lax.slice_in_dim(cells, 0, width, axis=dim)
        tail = lax.slice_in_dim(cells, cells.shape[dim] - width, cells.shape[dim], axis=dim)
        cells = jnp.concatenate(
            [
                lax.ppermute(tail, axis, [(i, (i + 1) % count) for i in range(ends)]),
                cells,
                lax.ppermute(head, axis, [((i + 1) % count, i) for i in range(ends)]),
            ],
            axis=dim,
        )
    return cells


def gathered(rows, axis):
    count = lax.axis_size(axis)
    position = lax.axis_index(axis)
    bit = 1
    while bit < count:
        other = lax.ppermute(rows, axis, [(i, i ^ bit) for i in range(count)])
        upper = (position & bit) != 0
        rows = jnp.concatenate(
            [jnp.where(upper, other, rows), jnp.where(upper, rows, other)], axis=0
        )
        bit *= 2
    return rows


def shift_table(length, tap_count):
    offset = np.arange(length + tap_count)[None, :] - np.arange(length)[:, None]
    table = (offset[None, :, :] == np.arange(tap_count)[:, None, None]).astype(np.float32)
    return jnp.asarray(table, jnp.bfloat16)


def banded(filters, table):
    return jnp.einsum("rt,toi->roi", filters, table, preferred_element_type=jnp.float32).astype(
        jnp.bfloat16
    )


def blur_slot(extended, factor_panel, tables, size_x, size_y, size_z):
    filters = factor_panel.reshape(R, 3, K)
    summed = jnp.zeros((size_x, size_y, size_z), jnp.float32)
    for rank_group in range(R // 4):
        chosen = filters[4 * rank_group : 4 * rank_group + 4]
        line_x = jnp.einsum(
            "roi,iyz->royz",
            banded(chosen[:, 0], tables[0]),
            extended,
            preferred_element_type=jnp.float32,
        ).astype(jnp.bfloat16)
        line_y = jnp.einsum(
            "roi,rxiz->rxoz",
            banded(chosen[:, 1], tables[1]),
            line_x,
            preferred_element_type=jnp.float32,
        ).astype(jnp.bfloat16)
        summed = summed + jnp.einsum(
            "roi,rxyi->xyo",
            banded(chosen[:, 2], tables[2]),
            line_y,
            preferred_element_type=jnp.float32,
        )
    return summed


def per_device(reflect, weights, cell_slot, factors, reader_list):
    half_width = K // 2
    size_x, size_y, size_z = reflect.shape
    rounded = reflect.astype(jnp.bfloat16)
    extended = padded(rounded, (("gz", 2), ("il", 0), ("xl", 1)), half_width)
    tables = (shift_table(size_x, K), shift_table(size_y, K), shift_table(size_z, K))
    listed = reader_list.reshape(NEED)
    live_mask = listed >= 0
    live_count = jnp.sum(live_mask.astype(jnp.int32))
    cross_count = lax.axis_size("xl")
    depth_count = lax.axis_size("gz")
    owner_index = jnp.where(live_mask, listed // (CP_DEV * depth_count) % cross_count, 0)
    local_row = jnp.where(live_mask, listed % CP_DEV, 0)
    panel_table = gathered(factors, "xl")
    row_key = owner_index * CP_DEV + local_row
    row_pick = (jnp.arange(cross_count * CP_DEV)[None, :] == row_key[:, None]) & live_mask[:, None]
    panels = jnp.dot(
        row_pick.astype(jnp.bfloat16), panel_table, preferred_element_type=jnp.float32
    ).astype(jnp.bfloat16)

    def add_slot(slot_index, blurred_sum):
        factor_panel = lax.dynamic_index_in_dim(panels, slot_index, 0, keepdims=False)
        weight_map = jnp.sum(
            jnp.where(cell_slot == slot_index, weights.astype(jnp.float32), 0.0), axis=0
        )
        return blurred_sum + weight_map * blur_slot(
            extended, factor_panel, tables, size_x, size_y, size_z
        )

    return lax.fori_loop(
        jnp.zeros((), jnp.int32),
        live_count,
        add_slot,
        jnp.zeros((size_x, size_y, size_z), jnp.float32),
    )


def solution(mesh):
    in_specs = (
        P("il", "xl", "gz"),
        P(None, "il", "xl", "gz"),
        P(None, "il", "xl", "gz"),
        P(("il", "xl", "gz"), None),
        P("il", "xl", "gz", None),
    )
    out_specs = P("il", "xl", "gz")
    return jax.shard_map(
        per_device, mesh=mesh, in_specs=in_specs, out_specs=out_specs, check_vma=False
    )
```

```python
import jax
import jax.numpy as jnp
import numpy as np
from jax import lax
from jax.experimental import pallas as pl
from jax.experimental.pallas import tpu as pltpu
from jax.sharding import PartitionSpec as P

K = 64
R = 8
CP_DEV = 4
NEED = 3
HALF = 32
X, Y, Z = 40, 40, 128
XB = X // 8
EXT = 104
GROUPS = EXT // 4
ROWS = 2 * EXT
NARROW = 128
TOP = 32


def x_table():
    table = np.zeros((K, XB, 2, 8, 2, EXT), np.float32)
    for b in range(XB):
        for o in range(8):
            for t in range(K):
                for s in range(2):
                    table[t, b, s, o, s, b * 8 + o + t] = 1
    return jnp.asarray(table.reshape(K, XB * 16, ROWS), jnp.bfloat16)


def y_table(first, count, low, high):
    table = np.zeros((K, count, high - low, 8), np.float32)
    for o in range(count):
        for t in range(K):
            table[t, o, first + o + t - low, :] = 1
    return jnp.asarray(table.reshape(K, count, (high - low) * 8), jnp.bfloat16)


def z_table():
    table = np.zeros((K, Z + 2 * HALF, Z), np.float32)
    for o in range(Z):
        for t in range(K):
            i = o + t
            place = i - HALF if HALF <= i < HALF + Z else (Z + i if i < HALF else i)
            table[t, place, o] = 1
    return jnp.asarray(table, jnp.bfloat16)


def spread(filters, table):
    return jnp.einsum("rt,tmk->rmk", filters, table, preferred_element_type=jnp.float32).astype(
        jnp.bfloat16
    )


def same_lane(columns):
    return jnp.asarray(np.arange(columns)[None, :] % 8 == np.arange(8)[:, None], jnp.bfloat16)


def roll_half(value):
    return pltpu.roll(value, 64, 1)


def blur_kernel(
    live_ref, left_ref, own_ref, right_ref, a1_ref, a2_ref, a2b_ref, mask_ref, bz_ref,
    weights_ref, slot_ref, out_ref, line_x, line_y, band_y,
):
    out_ref[...] = jnp.zeros_like(out_ref)
    low_x = lax.broadcasted_iota(jnp.int32, (16, NARROW), 1) < 64
    low_y = lax.broadcasted_iota(jnp.int32, (256, NARROW), 1) < 64
    low_b = lax.broadcasted_iota(jnp.int32, (64, NARROW), 1) < 64

    def one_slot(slot, carry):
        def stage_x(part, offset):
            def step(i, carry):
                g = 2 * i
                rhs = jnp.concatenate(
                    [part[g, 0], part[g, 1], part[g + 1, 0], part[g + 1, 1], part[g, 2], part[g + 1, 2]],
                    axis=1,
                )
                made = jnp.dot(a1_ref[slot], rhs, preferred_element_type=jnp.float32)
                base = pl.multiple_of((offset + g) * 32, 64)
                for r in range(R):
                    for b in range(XB):
                        rows = slice((r * XB + b) * 16, (r * XB + b + 1) * 16)
                        for k in range(4):
                            line_x[r, pl.ds(base + k * 16, 16), b * 128 : (b + 1) * 128] = made[
                                rows, k * 128 : (k + 1) * 128
                            ].astype(jnp.bfloat16)
                    for k in range(2):
                        tails = [
                            made[(r * XB + b) * 16 : (r * XB + b + 1) * 16, 512 + k * 128 : 640 + k * 128]
                            for b in range(XB)
                        ]
                        turned = [roll_half(t) for t in tails]
                        at = pl.ds(base + k * 32, 16)
                        after = pl.ds(base + k * 32 + 16, 16)
                        for c in range(2):
                            lanes = slice((5 + c) * 128, (6 + c) * 128)
                            line_x[r, at, lanes] = jnp.where(low_x, tails[2 * c], turned[2 * c + 1]).astype(jnp.bfloat16)
                            line_x[r, after, lanes] = jnp.where(low_x, turned[2 * c], tails[2 * c + 1]).astype(jnp.bfloat16)
                        lanes = slice(7 * 128, 8 * 128)
                        line_x[r, at, lanes] = (tails[4] if r % 2 == 0 else turned[4]).astype(jnp.bfloat16)
                        line_x[r, after, lanes] = (turned[4] if r % 2 == 0 else tails[4]).astype(jnp.bfloat16)
                return carry

            lax.fori_loop(0, part.shape[0] // 2, step, 0)

        stage_x(left_ref, 0)
        stage_x(own_ref, 8)
        stage_x(right_ref, 18)

        def pair(q, carry):
            tops, ends = [], []
            for h in range(2):
                r = 2 * q + h
                top = a2_ref[slot * R + r]
                for o in range(8):
                    band_y[h, o * TOP : (o + 1) * TOP, :] = top * mask_ref[o : o + 1, :]
                tops.append(jnp.dot(band_y[h], line_x[r, 0:768, :], preferred_element_type=jnp.float32))
                ends.append(jnp.dot(a2b_ref[slot * R + r], line_x[r, 256:832, :], preferred_element_type=jnp.float32))
            for made, count, start, low in ((tops, 256, 0, low_y), (ends, 64, 1280, low_b)):
                lanes = pl.multiple_of(q * 384, 128)
                for b in range(XB):
                    rows = slice(start + b * count, start + (b + 1) * count)
                    for h in range(2):
                        line_y[rows, pl.ds(lanes + h * 128, 128)] = made[h][:, b * 128 : (b + 1) * 128].astype(jnp.bfloat16)
                tail = pl.ds(lanes + 256, 128)
                for c in range(2):
                    first = made[0][:, (5 + c) * 128 : (6 + c) * 128]
                    second = made[1][:, (5 + c) * 128 : (6 + c) * 128]
                    rows = slice(start + 2 * c * count, start + (2 * c + 1) * count)
                    line_y[rows, tail] = jnp.where(low, first, roll_half(second)).astype(jnp.bfloat16)
                    rows = slice(start + (2 * c + 1) * count, start + (2 * c + 2) * count)
                    line_y[rows, tail] = jnp.where(low, roll_half(first), second).astype(jnp.bfloat16)
                rows = slice(start + 4 * count, start + 5 * count)
                line_y[rows, tail] = jnp.where(low, made[0][:, 896:1024], made[1][:, 896:1024]).astype(jnp.bfloat16)
            return carry

        lax.fori_loop(0, R // 2, pair, 0)

        done = jnp.dot(line_y[...], bz_ref[slot], preferred_element_type=jnp.float32)
        for low, high, made in ((0, TOP, done[:1280]), (TOP, Y, done[1280:])):
            weight = jnp.zeros((X, high - low, Z), jnp.float32)
            for j in range(2):
                here = slot_ref[j, :, low:high, :] == slot
                weight = weight + jnp.where(here, weights_ref[j, :, low:high, :].astype(jnp.float32), 0.0)
            out_ref[:, low:high, :] += weight * made.reshape(X, high - low, Z)
        return carry

    lax.fori_loop(0, live_ref[0], one_slot, 0)


def blur(live, left, own, right, bands, weights, cell_slot):
    a1, a2, a2b, bz = bands
    vmem = pl.BlockSpec(memory_space=pltpu.VMEM)
    mask = same_lane(768)
    return pl.pallas_call(
        blur_kernel,
        out_shape=jax.ShapeDtypeStruct((X, Y, Z), jnp.float32),
        in_specs=[pl.BlockSpec(memory_space=pltpu.SMEM)] + [vmem] * 10,
        out_specs=vmem,
        scratch_shapes=[
            pltpu.VMEM((R, 832, 1024), jnp.bfloat16),
            pltpu.VMEM((1600, 1536), jnp.bfloat16),
            pltpu.VMEM((2, 256, 768), jnp.bfloat16),
        ],
        compiler_params=pltpu.CompilerParams(vmem_limit_bytes=60 * 1024 * 1024),
    )(live, left, own, right, a1, a2, a2b, mask, bz, weights, cell_slot)


def make_bands(panels):
    filters = panels.reshape(NEED * R, 3, K)
    a1 = spread(filters[:, 0], x_table()).reshape(NEED, R * XB * 16, ROWS)
    a2 = spread(filters[:, 1], y_table(0, TOP, 0, 96))
    ends = spread(filters[:, 1], y_table(TOP, Y - TOP, 32, 104))
    a2b = (ends[:, None] * same_lane(576)[None, :, None, :]).reshape(NEED * R, 64, 576)
    bz = spread(filters[:, 2], z_table()).reshape(NEED, R // 2, 2, Z + 2 * HALF, Z)
    bz = jnp.concatenate(
        [bz[:, :, 0, :Z], bz[:, :, 1, :Z], bz[:, :, 0, Z:], bz[:, :, 1, Z:]], axis=2
    ).reshape(NEED, R * (Z + 2 * HALF), Z)
    return a1, a2, a2b, bz


def gathered(rows, axis):
    count = lax.axis_size(axis)
    position = lax.axis_index(axis)
    bit = 1
    while bit < count:
        other = lax.ppermute(rows, axis, [(i, i ^ bit) for i in range(count)])
        upper = (position & bit) != 0
        rows = jnp.concatenate(
            [jnp.where(upper, other, rows), jnp.where(upper, rows, other)], axis=0
        )
        bit *= 2
    return rows


def both_ways(to_next, to_last, axis):
    count = lax.axis_size(axis)
    ends = count - 1
    return (
        lax.ppermute(to_next, axis, [(i, (i + 1) % count) for i in range(ends)]),
        lax.ppermute(to_last, axis, [((i + 1) % count, i) for i in range(ends)]),
    )


def halo(reflect):
    own = reflect.astype(jnp.bfloat16).transpose(1, 0, 2)
    parts = own.reshape(5, 2, 2, 2, X, Z)

    def packed(cells):
        return jnp.concatenate([cells[:, a, b] for a in range(2) for b in range(2)], axis=-1)

    left, right = both_ways(packed(parts[..., Z - HALF :]), packed(parts[..., :HALF]), "gz")
    tails = []
    for a in range(2):
        pieces = []
        for b in range(2):
            lanes = slice((2 * a + b) * HALF, (2 * a + b + 1) * HALF)
            pieces += [left[..., lanes], right[..., lanes]]
        tails.append(jnp.concatenate(pieces, axis=-1))
    tail = jnp.stack(tails, axis=1).reshape(10, 2, X, NARROW)
    block = jnp.concatenate([own.reshape(10, 4, X, Z), tail], axis=1)
    before, after = both_ways(block[:, :, X - HALF :], block[:, :, :HALF], "il")
    block = jnp.concatenate([before, block, after], axis=2).reshape(10, 3, ROWS, NARROW)
    left, right = both_ways(block[2:], block[:8], "xl")
    return left, block, right


def per_device(reflect, weights, cell_slot, factors, reader_list):
    listed = reader_list.reshape(NEED)
    live_mask = listed >= 0
    live_count = jnp.sum(live_mask.astype(jnp.int32))
    cross_count = lax.axis_size("xl")
    depth_count = lax.axis_size("gz")
    owner_index = jnp.where(live_mask, listed // (CP_DEV * depth_count) % cross_count, 0)
    local_row = jnp.where(live_mask, listed % CP_DEV, 0)
    panel_table = gathered(factors, "xl")
    row_key = owner_index * CP_DEV + local_row
    row_pick = (jnp.arange(cross_count * CP_DEV)[None, :] == row_key[:, None]) & live_mask[:, None]
    panels = jnp.dot(
        row_pick.astype(jnp.bfloat16), panel_table, preferred_element_type=jnp.float32
    ).astype(jnp.bfloat16)
    bands = make_bands(panels)
    left, own, right = halo(reflect)
    return blur(live_count.reshape(1), left, own, right, bands, weights, cell_slot)


def solution(mesh):
    in_specs = (
        P("il", "xl", "gz"),
        P(None, "il", "xl", "gz"),
        P(None, "il", "xl", "gz"),
        P(("il", "xl", "gz"), None),
        P("il", "xl", "gz", None),
    )
    out_specs = P("il", "xl", "gz")
    return jax.shard_map(
        per_device, mesh=mesh, in_specs=in_specs, out_specs=out_specs, check_vma=False
    )
```

```python
import jax
import jax.numpy as jnp
import numpy as np
from jax import lax
from jax.experimental import pallas as pl
from jax.experimental.pallas import tpu as pltpu
from jax.sharding import PartitionSpec as P

K = 64
R = 8
CP_DEV = 4
NEED = 3
HALF = 32
X, Y, Z = 40, 40, 128
XB = X // 8
EXT = 104
GROUPS = EXT // 4
ROWS = 2 * EXT
NARROW = 128
TOP = 32


def x_table():
    table = np.zeros((K, XB, 2, 8, ROWS), np.float32)
    for b in range(XB):
        for o in range(8):
            for t in range(K):
                x = b * 8 + o + t
                for start, count in ((0, HALF), (HALF, X), (HALF + X, HALF)):
                    if start <= x < start + count:
                        for s in range(2):
                            table[t, b, s, o, 2 * start + s * count + x - start] = 1
    return jnp.asarray(table.reshape(K, XB * 16, ROWS), jnp.bfloat16)


def y_table(first, count, low, high):
    table = np.zeros((K, count, high - low, 8), np.float32)
    for o in range(count):
        for t in range(K):
            table[t, o, first + o + t - low, :] = 1
    return jnp.asarray(table.reshape(K, count, (high - low) * 8), jnp.bfloat16)


def z_table():
    table = np.zeros((K, Z + 2 * HALF, Z), np.float32)
    for o in range(Z):
        for t in range(K):
            i = o + t
            place = i - HALF if HALF <= i < HALF + Z else (Z + i if i < HALF else i)
            table[t, place, o] = 1
    return jnp.asarray(table, jnp.bfloat16)


def spread(filters, table):
    return jnp.einsum("rt,tmk->rmk", filters, table, preferred_element_type=jnp.float32).astype(
        jnp.bfloat16
    )


def same_lane(columns):
    return jnp.asarray(np.arange(columns)[None, :] % 8 == np.arange(8)[:, None], jnp.bfloat16)


def roll_half(value):
    return pltpu.roll(value, 64, 1)


def blur_kernel(
    live_ref, left_ref, own_ref, right_ref, left_tail, own_tail, right_tail, a1_ref, a2_ref, a2b_ref, mask_ref, bz_ref,
    weights_ref, slot_ref, out_ref, line_x, line_y, band_y,
):
    out_ref[...] = jnp.zeros_like(out_ref)
    low_x = lax.broadcasted_iota(jnp.int32, (16, NARROW), 1) < 64
    low_y = lax.broadcasted_iota(jnp.int32, (256, NARROW), 1) < 64
    low_b = lax.broadcasted_iota(jnp.int32, (64, NARROW), 1) < 64

    def one_slot(slot, carry):
        def stage_x(part, tail, offset):
            def step(i, carry):
                g = 2 * i
                rhs = jnp.concatenate(
                    [part[4 * i], part[4 * i + 1], part[4 * i + 2], part[4 * i + 3], tail[g], tail[g + 1]],
                    axis=1,
                )
                made = jnp.dot(a1_ref[slot], rhs, preferred_element_type=jnp.float32)
                base = pl.multiple_of((offset + g) * 32, 64)
                for r in range(R):
                    for b in range(XB):
                        rows = slice((r * XB + b) * 16, (r * XB + b + 1) * 16)
                        for k in range(4):
                            line_x[r, pl.ds(base + k * 16, 16), b * 128 : (b + 1) * 128] = made[
                                rows, k * 128 : (k + 1) * 128
                            ].astype(jnp.bfloat16)
                    for k in range(2):
                        tails = [
                            made[(r * XB + b) * 16 : (r * XB + b + 1) * 16, 512 + k * 128 : 640 + k * 128]
                            for b in range(XB)
                        ]
                        turned = [roll_half(t) for t in tails]
                        at = pl.ds(base + k * 32, 16)
                        after = pl.ds(base + k * 32 + 16, 16)
                        for c in range(2):
                            lanes = slice((5 + c) * 128, (6 + c) * 128)
                            line_x[r, at, lanes] = jnp.where(low_x, tails[2 * c], turned[2 * c + 1]).astype(jnp.bfloat16)
                            line_x[r, after, lanes] = jnp.where(low_x, turned[2 * c], tails[2 * c + 1]).astype(jnp.bfloat16)
                        lanes = slice(7 * 128, 8 * 128)
                        line_x[r, at, lanes] = (tails[4] if r % 2 == 0 else turned[4]).astype(jnp.bfloat16)
                        line_x[r, after, lanes] = (turned[4] if r % 2 == 0 else tails[4]).astype(jnp.bfloat16)
                return carry

            lax.fori_loop(0, part.shape[0] // 4, step, 0)

        stage_x(left_ref, left_tail, 0)
        stage_x(own_ref, own_tail, 8)
        stage_x(right_ref, right_tail, 18)

        def pair(q, carry):
            tops, ends = [], []
            for h in range(2):
                r = 2 * q + h
                top = a2_ref[slot * R + r]
                for o in range(8):
                    band_y[h, o * TOP : (o + 1) * TOP, :] = top * mask_ref[o : o + 1, :]
                tops.append(jnp.dot(band_y[h], line_x[r, 0:768, :], preferred_element_type=jnp.float32))
                ends.append(jnp.dot(a2b_ref[slot * R + r], line_x[r, 256:832, :], preferred_element_type=jnp.float32))
            for made, count, start, low in ((tops, 256, 0, low_y), (ends, 64, 1280, low_b)):
                lanes = pl.multiple_of(q * 384, 128)
                for b in range(XB):
                    rows = slice(start + b * count, start + (b + 1) * count)
                    for h in range(2):
                        line_y[rows, pl.ds(lanes + h * 128, 128)] = made[h][:, b * 128 : (b + 1) * 128].astype(jnp.bfloat16)
                tail = pl.ds(lanes + 256, 128)
                for c in range(2):
                    first = made[0][:, (5 + c) * 128 : (6 + c) * 128]
                    second = made[1][:, (5 + c) * 128 : (6 + c) * 128]
                    rows = slice(start + 2 * c * count, start + (2 * c + 1) * count)
                    line_y[rows, tail] = jnp.where(low, first, roll_half(second)).astype(jnp.bfloat16)
                    rows = slice(start + (2 * c + 1) * count, start + (2 * c + 2) * count)
                    line_y[rows, tail] = jnp.where(low, roll_half(first), second).astype(jnp.bfloat16)
                rows = slice(start + 4 * count, start + 5 * count)
                line_y[rows, tail] = jnp.where(low, made[0][:, 896:1024], made[1][:, 896:1024]).astype(jnp.bfloat16)
            return carry

        lax.fori_loop(0, R // 2, pair, 0)

        done = jnp.dot(line_y[...], bz_ref[slot], preferred_element_type=jnp.float32)
        for low, high, made in ((0, TOP, done[:1280]), (TOP, Y, done[1280:])):
            weight = jnp.zeros((X, high - low, Z), jnp.float32)
            for j in range(2):
                here = slot_ref[j, :, low:high, :] == slot
                weight = weight + jnp.where(here, weights_ref[j, :, low:high, :].astype(jnp.float32), 0.0)
            out_ref[:, low:high, :] += weight * made.reshape(X, high - low, Z)
        return carry

    lax.fori_loop(0, live_ref[0], one_slot, 0)


def blur(live, cells, bands, weights, cell_slot):
    a1, a2, a2b, bz = bands
    vmem = pl.BlockSpec(memory_space=pltpu.VMEM)
    mask = same_lane(768)
    return pl.pallas_call(
        blur_kernel,
        out_shape=jax.ShapeDtypeStruct((X, Y, Z), jnp.float32),
        in_specs=[pl.BlockSpec(memory_space=pltpu.SMEM)] + [vmem] * 13,
        out_specs=vmem,
        scratch_shapes=[
            pltpu.VMEM((R, 832, 1024), jnp.bfloat16),
            pltpu.VMEM((1600, 1536), jnp.bfloat16),
            pltpu.VMEM((2, 256, 768), jnp.bfloat16),
        ],
        compiler_params=pltpu.CompilerParams(vmem_limit_bytes=60 * 1024 * 1024),
    )(live, *cells, a1, a2, a2b, mask, bz, weights, cell_slot)


def make_bands(panels):
    filters = panels.reshape(NEED * R, 3, K)
    a1 = spread(filters[:, 0], x_table()).reshape(NEED, R * XB * 16, ROWS)
    a2 = spread(filters[:, 1], y_table(0, TOP, 0, 96))
    ends = spread(filters[:, 1], y_table(TOP, Y - TOP, 32, 104))
    a2b = (ends[:, None] * same_lane(576)[None, :, None, :]).reshape(NEED * R, 64, 576)
    bz = spread(filters[:, 2], z_table()).reshape(NEED, R // 2, 2, Z + 2 * HALF, Z)
    bz = jnp.concatenate(
        [bz[:, :, 0, :Z], bz[:, :, 1, :Z], bz[:, :, 0, Z:], bz[:, :, 1, Z:]], axis=2
    ).reshape(NEED, R * (Z + 2 * HALF), Z)
    return a1, a2, a2b, bz


def gathered(rows, axis):
    count = lax.axis_size(axis)
    position = lax.axis_index(axis)
    bit = 1
    while bit < count:
        other = lax.ppermute(rows, axis, [(i, i ^ bit) for i in range(count)])
        upper = (position & bit) != 0
        rows = jnp.concatenate(
            [jnp.where(upper, other, rows), jnp.where(upper, rows, other)], axis=0
        )
        bit *= 2
    return rows


def both_ways(to_next, to_last, axis):
    count = lax.axis_size(axis)
    ends = count - 1
    return (
        lax.ppermute(to_next, axis, [(i, (i + 1) % count) for i in range(ends)]),
        lax.ppermute(to_last, axis, [((i + 1) % count, i) for i in range(ends)]),
    )


def lane_part():
    return lax.broadcasted_iota(jnp.int32, (1, NARROW), 1) // HALF


def cut_kernel(reflect_ref, own_ref, next_ref, last_ref, deeper_ref, shallower_ref):
    part = lane_part()
    for g in range(Y // 8):
        rows = [reflect_ref[:, 8 * g + k, :] for k in range(8)]
        for pair in range(4):
            two = rows[2 * pair : 2 * pair + 2]
            own_ref[4 * g + pair] = jnp.concatenate(two, axis=0).astype(jnp.bfloat16)
            next_ref[4 * g + pair] = jnp.concatenate([v[X - HALF :] for v in two], axis=0).astype(jnp.bfloat16)
            last_ref[4 * g + pair] = jnp.concatenate([v[:HALF] for v in two], axis=0).astype(jnp.bfloat16)
        for ref, first in ((deeper_ref, Z - HALF), (shallower_ref, 0)):
            packed = []
            for s in range(2):
                value = None
                for k in range(4):
                    shift = (k * HALF - first) % NARROW
                    turned = rows[2 * k + s]
                    turned = pltpu.roll(turned, shift, 1) if shift else turned
                    value = turned if value is None else jnp.where(part == k, turned, value)
                packed.append(value)
            ref[g] = jnp.concatenate(packed, axis=0).astype(jnp.bfloat16)


def cut(reflect):
    shapes = [(20, 80, Z), (20, 64, Z), (20, 64, Z), (5, 80, NARROW), (5, 80, NARROW)]
    vmem = pl.BlockSpec(memory_space=pltpu.VMEM)
    return pl.pallas_call(
        cut_kernel,
        out_shape=[jax.ShapeDtypeStruct(shape, jnp.bfloat16) for shape in shapes],
        in_specs=[vmem],
        out_specs=[vmem] * 5,
    )(reflect)


def tail_kernel(left_ref, right_ref, after_ref, own_ref, next_ref, last_ref):
    part = lane_part()
    for g in range(5):
        left = left_ref[g].astype(jnp.float32)
        right = right_ref[g].astype(jnp.float32)
        for a in range(2):
            value = left if a == 0 else pltpu.roll(left, 64, 1)
            for k, (source, at) in enumerate(((right, 2 * a), (left, 2 * a + 1), (right, 2 * a + 1)), 1):
                shift = ((k - at) * HALF) % NARROW
                turned = pltpu.roll(source, shift, 1) if shift else source
                value = jnp.where(part == k, turned, value)
            own_ref[2 * g + a] = value.astype(jnp.bfloat16)
            next_ref[2 * g + a] = jnp.concatenate(
                [value[X - HALF : X], value[2 * X - HALF :]], axis=0
            ).astype(jnp.bfloat16)
            last_ref[2 * g + a] = jnp.concatenate(
                [value[:HALF], value[X : X + HALF]], axis=0
            ).astype(jnp.bfloat16)


def unpack_tail(left, right, after):
    shapes = [(10, 80, NARROW), (10, 64, NARROW), (10, 64, NARROW)]
    vmem = pl.BlockSpec(memory_space=pltpu.VMEM)
    return pl.pallas_call(
        tail_kernel,
        out_shape=[jax.ShapeDtypeStruct(shape, jnp.bfloat16) for shape in shapes],
        in_specs=[vmem, vmem, pl.BlockSpec(memory_space=pl.ANY)],
        out_specs=[vmem] * 3,
    )(left, right, after)


def join_kernel(before_ref, own_ref, after_ref, all_ref, next_ref, last_ref):
    count = own_ref.shape[0]
    edge = next_ref.shape[0]
    for ref, start in ((all_ref, 0), (next_ref, count - edge), (last_ref, 0)):
        rows = slice(start, start + ref.shape[0])
        ref[:, 0:64, :] = before_ref[rows]
        ref[:, 64:144, :] = own_ref[rows]
        ref[:, 144:208, :] = after_ref[rows]


def join(before, own, after):
    count = own.shape[0]
    counts = (count, count * 4 // 5, count * 4 // 5)
    vmem = pl.BlockSpec(memory_space=pltpu.VMEM)
    return pl.pallas_call(
        join_kernel,
        out_shape=[jax.ShapeDtypeStruct((n, ROWS, NARROW), jnp.bfloat16) for n in counts],
        in_specs=[vmem] * 3,
        out_specs=[vmem] * 3,
        compiler_params=pltpu.CompilerParams(vmem_limit_bytes=32 * 1024 * 1024),
    )(before, own, after)


def halo(reflect):
    own, to_next, to_last, deeper, shallower = cut(reflect)
    above, below = both_ways(deeper, shallower, "gz")
    before, after = both_ways(to_next, to_last, "il")
    main, to_next, to_last = join(before, own, after)
    left, right = both_ways(to_next, to_last, "xl")
    tail, to_next, to_last = unpack_tail(above, below, main)
    before, after = both_ways(to_next, to_last, "il")
    tail, to_next, to_last = join(before, tail, after)
    left_tail, right_tail = both_ways(to_next, to_last, "xl")
    return left, main, right, left_tail, tail, right_tail


def per_device(reflect, weights, cell_slot, factors, reader_list):
    listed = reader_list.reshape(NEED)
    live_mask = listed >= 0
    live_count = jnp.sum(live_mask.astype(jnp.int32))
    cross_count = lax.axis_size("xl")
    depth_count = lax.axis_size("gz")
    owner_index = jnp.where(live_mask, listed // (CP_DEV * depth_count) % cross_count, 0)
    local_row = jnp.where(live_mask, listed % CP_DEV, 0)
    panel_table = gathered(factors, "xl")
    row_key = owner_index * CP_DEV + local_row
    row_pick = (jnp.arange(cross_count * CP_DEV)[None, :] == row_key[:, None]) & live_mask[:, None]
    panels = jnp.dot(
        row_pick.astype(jnp.bfloat16), panel_table, preferred_element_type=jnp.float32
    ).astype(jnp.bfloat16)
    bands = make_bands(panels)
    return blur(live_count.reshape(1), halo(reflect), bands, weights, cell_slot)


def solution(mesh):
    in_specs = (
        P("il", "xl", "gz"),
        P(None, "il", "xl", "gz"),
        P(None, "il", "xl", "gz"),
        P(("il", "xl", "gz"), None),
        P("il", "xl", "gz", None),
    )
    out_specs = P("il", "xl", "gz")
    return jax.shard_map(
        per_device, mesh=mesh, in_specs=in_specs, out_specs=out_specs, check_vma=False
    )
```

```python
import jax
import jax.numpy as jnp
import numpy as np
from jax import lax
from jax.experimental import pallas as pl
from jax.experimental.pallas import tpu as pltpu
from jax.sharding import PartitionSpec as P

K = 64
R = 8
CP_DEV = 4
NEED = 3
HALF = 32
X, Y, Z = 40, 40, 128
XO = 4
XB = X // XO
LANES = XB * 192
EXT = 104
ROWS = 2 * EXT
NARROW = 128
TOP = 32


def same_lane():
    return jnp.asarray(np.arange(EXT * XO)[None, :] % XO == np.arange(XO)[:, None], jnp.bfloat16)


def tap_maps():
    reverse = np.zeros((128, 128), np.float32)
    repeat = np.zeros((128, 256), np.float32)
    for t in range(K):
        reverse[t, -t % 128] = 1
        repeat[t, XO * t : XO * (t + 1)] = 1
    return jnp.asarray(np.concatenate([reverse, repeat], axis=1), jnp.bfloat16)


def bands_kernel(list_ref, table_ref, map_ref, a1_ref, a2_ref, a2b_ref, bz_ref, table, taps, long):
    for tile in range(12):
        table[tile] = table_ref[:, tile * 128 : (tile + 1) * 128].astype(jnp.float32)
    lane = lax.broadcasted_iota(jnp.int32, (1, 128), 1)
    for slot in range(NEED):
        listed = jnp.maximum(list_ref[slot], 0)
        key = (listed // (CP_DEV * 8)) % 8 * CP_DEV + listed % CP_DEV
        for r in range(R):
            for axis in range(3):
                tile, half = divmod(3 * r + axis, 2)
                piece = table[tile, pl.ds(key, 1), :]
                if half:
                    piece = pltpu.roll(piece, 64, 1)
                at = axis * NEED * R + slot * R + r
                taps[at : at + 1, :] = jnp.where(lane < K, piece, 0.0)
    mapped = jnp.dot(
        taps[...].astype(jnp.bfloat16), map_ref[...], preferred_element_type=jnp.float32
    )
    for tile in range(3):
        long[tile] = mapped[:, tile * 128 : (tile + 1) * 128]

    row8 = lax.broadcasted_iota(jnp.int32, (8, 128), 0)
    lane8 = lax.broadcasted_iota(jnp.int32, (8, 128), 1)
    low = row8 < 4

    def between(first, last):
        return (lane8 >= first) & (lane8 < last)

    plain = low & between(0, 32)
    by_32 = (low & between(64, 104)) | (~low & between(32, 64))
    by_72 = ~low & between(104, 128)
    end_72 = (low & between(16, 48)) | (~low & between(0, 16))
    end_104 = ~low & between(48, 80)
    row_z = lax.broadcasted_iota(jnp.int32, (128, 128), 0)
    lane_z = lax.broadcasted_iota(jnp.int32, (128, 128), 1)
    inside = lane_z <= row_z
    row_y = lax.broadcasted_iota(jnp.int32, (TOP, 128), 0)
    lane_y = lax.broadcasted_iota(jnp.int32, (TOP, 128), 1)
    after = lane_y >= XO * row_y
    after8 = lane8 >= XO * row8

    def one_term(i, carry):
        slot = i // R
        r = i % R
        row = jnp.broadcast_to(taps[pl.ds(i, 1), :], (8, 128))
        base = pltpu.roll(row, 0, 1, stride=1, stride_axis=0)
        base = jnp.where(low, base, pltpu.roll(base, 124, 1))
        for b in range(0, XB, 2):
            ends = ([], [])
            for c in (b, b + 1):
                turned = [
                    pltpu.roll(base, (XO * c + k) % 128, 1) if (XO * c + k) % 128 else base
                    for k in (0, 32, 72, 104)
                ]
                ends[0].append(
                    jnp.where(plain, turned[0], jnp.where(by_32, turned[1], jnp.where(by_72, turned[2], 0.0)))
                )
                ends[1].append(jnp.where(end_72, turned[2], jnp.where(end_104, turned[3], 0.0)))
            rows = pl.ds(pl.multiple_of(r * (XB * 8) + b * 8, 16), 16)
            a1_ref[slot, rows, 0:128] = jnp.concatenate(ends[0], axis=0).astype(jnp.bfloat16)
            a1_ref[slot, rows, 128:ROWS] = jnp.concatenate(ends[1], axis=0)[:, : ROWS - 128].astype(jnp.bfloat16)
        halves = [
            pltpu.roll(
                jnp.broadcast_to(long[k, pl.ds(NEED * R + i, 1), :], (TOP, 128)),
                0, 1, stride=XO, stride_axis=0,
            )
            for k in (1, 2)
        ]
        zero = jnp.zeros((TOP, 128), jnp.float32)
        tiles = [
            jnp.where(after, halves[0], 0.0),
            jnp.where(after, halves[1], halves[0]),
            jnp.where(after, 0.0, halves[1]),
            zero,
        ]
        for k in range(4):
            width = min(128, EXT * XO - 128 * k)
            a2_ref[i, :, 128 * k : 128 * k + width] = tiles[k][:, :width].astype(jnp.bfloat16)
        ends = [
            jnp.zeros((8, 128), jnp.float32),
            jnp.where(after8, halves[0][:8], 0.0),
            jnp.where(after8, halves[1][:8], halves[0][:8]),
            jnp.where(after8, 0.0, halves[1][:8]),
        ]
        for k in range(4):
            width = min(128, EXT * XO - 128 * k)
            for o in range(0, XO, 2):
                two = jnp.concatenate(
                    [jnp.where(lane8 % XO == c, ends[k], 0.0) for c in (o, o + 1)], axis=0
                )
                a2b_ref[i, 8 * o : 8 * o + 16, 128 * k : 128 * k + width] = two[:, :width].astype(jnp.bfloat16)
        row = jnp.broadcast_to(long[0, pl.ds(2 * NEED * R + i, 1), :], (128, 128))
        turned = pltpu.roll(row, 0, 1, stride=1, stride_axis=0)
        first = jnp.where(inside, turned, 0.0).astype(jnp.bfloat16)
        second = jnp.where(inside, 0.0, turned).astype(jnp.bfloat16)
        start = (r // 2) * (2 * (Z + 2 * HALF))
        own = pl.multiple_of(start + (r % 2) * Z, 128)
        bz_ref[slot, pl.ds(own, 96), :] = first[32:]
        bz_ref[slot, pl.ds(own + 96, 32), :] = second[:32]
        ends = pl.multiple_of(start + 2 * Z + (r % 2) * 2 * HALF, 64)
        bz_ref[slot, pl.ds(ends, 32), :] = first[:32]
        bz_ref[slot, pl.ds(ends + 32, 32), :] = second[32:64]
        return carry

    lax.fori_loop(0, NEED * R, one_term, 0)


def make_bands(listed, table):
    shapes = [
        (NEED, R * XB * 8, ROWS),
        (NEED * R, TOP, EXT * XO),
        (NEED * R, XO * (Y - TOP), EXT * XO),
        (NEED, R * (Z + 2 * HALF), Z),
    ]
    vmem = pl.BlockSpec(memory_space=pltpu.VMEM)
    return pl.pallas_call(
        bands_kernel,
        out_shape=[jax.ShapeDtypeStruct(shape, jnp.bfloat16) for shape in shapes],
        in_specs=[pl.BlockSpec(memory_space=pltpu.SMEM), vmem, vmem],
        out_specs=[vmem] * 4,
        scratch_shapes=[
            pltpu.VMEM((12, 32, 128), jnp.float32),
            pltpu.VMEM((3 * NEED * R, 128), jnp.float32),
            pltpu.VMEM((3, 3 * NEED * R, 128), jnp.float32),
        ],
        compiler_params=pltpu.CompilerParams(vmem_limit_bytes=32 * 1024 * 1024),
    )(listed, table, tap_maps())


def roll_half(value):
    return pltpu.roll(value, 64, 1)


def blur_kernel(
    live_ref, left_ref, own_ref, right_ref, left_tail, own_tail, right_tail, a1_ref, a2_ref, a2b_ref, mask_ref, bz_ref,
    weights_ref, slot_ref, out_ref, line_x, line_y, band_y,
):
    out_ref[...] = jnp.zeros_like(out_ref)
    low_x = lax.broadcasted_iota(jnp.int32, (8, NARROW), 1) < 64
    low_y = lax.broadcasted_iota(jnp.int32, (TOP * XO, NARROW), 1) < 64
    low_b = lax.broadcasted_iota(jnp.int32, ((Y - TOP) * XO, NARROW), 1) < 64

    def one_slot(slot, carry):
        def stage_x(part, tail, offset):
            def step(i, carry):
                g = 2 * i
                rhs = jnp.concatenate(
                    [part[4 * i], part[4 * i + 1], part[4 * i + 2], part[4 * i + 3], tail[g], tail[g + 1]],
                    axis=1,
                )
                made = jnp.dot(a1_ref[slot], rhs, preferred_element_type=jnp.float32)
                base = pl.multiple_of((offset + g) * 16, 32)

                def cell(r, b, k):
                    row = (r * XB + b) * 8
                    return made[row : row + 8, k * 128 : (k + 1) * 128]

                def put(r, k, column, first, second):
                    line_x[r, pl.ds(base + k * 16, 16), column * 128 : (column + 1) * 128] = (
                        jnp.concatenate([first, second], axis=0).astype(jnp.bfloat16)
                    )

                for r in range(R):
                    for k in range(2):
                        for b in range(XB):
                            put(r, k, b, cell(r, b, 2 * k), cell(r, b, 2 * k + 1))
                        for c in range(XB // 2):
                            one, two = cell(r, 2 * c, 4 + k), cell(r, 2 * c + 1, 4 + k)
                            put(
                                r, k, XB + c,
                                jnp.where(low_x, one, roll_half(two)),
                                jnp.where(low_x, roll_half(one), two),
                            )
                return carry

            lax.fori_loop(0, part.shape[0] // 4, step, 0)

        stage_x(left_ref, left_tail, 0)
        stage_x(own_ref, own_tail, 8)
        stage_x(right_ref, right_tail, 18)

        def pair(q, carry):
            made = []
            for h in range(2):
                r = 2 * q + h
                top = a2_ref[slot * R + r]
                for o in range(XO):
                    band_y[h, o * TOP : (o + 1) * TOP, :] = top * mask_ref[o : o + 1, :]
                band_y[h, TOP * XO :, :] = a2b_ref[slot * R + r]
                made.append(jnp.dot(band_y[h], line_x[r], preferred_element_type=jnp.float32))
            lanes = pl.multiple_of(q * 384, 128)
            tail = pl.ds(lanes + 256, 128)
            for first, count, start, low in ((0, TOP * XO, 0, low_y), (TOP * XO, (Y - TOP) * XO, TOP * X, low_b)):

                def cell(h, column):
                    return made[h][first : first + count, column * 128 : (column + 1) * 128]

                def rows(b):
                    return slice(start + b * count, start + (b + 1) * count)

                for b in range(XB):
                    for h in range(2):
                        line_y[rows(b), pl.ds(lanes + h * 128, 128)] = cell(h, b).astype(jnp.bfloat16)
                for c in range(XB // 2):
                    one, two = cell(0, XB + c), cell(1, XB + c)
                    line_y[rows(2 * c), tail] = jnp.where(low, one, roll_half(two)).astype(jnp.bfloat16)
                    line_y[rows(2 * c + 1), tail] = jnp.where(low, roll_half(one), two).astype(jnp.bfloat16)
            return carry

        lax.fori_loop(0, R // 2, pair, 0)

        done = jnp.dot(line_y[...], bz_ref[slot], preferred_element_type=jnp.float32)
        for low, high, made in ((0, TOP, done[:1280]), (TOP, Y, done[1280:])):
            weight = jnp.zeros((X, high - low, Z), jnp.float32)
            for j in range(2):
                here = slot_ref[j, :, low:high, :] == slot
                weight = weight + jnp.where(here, weights_ref[j, :, low:high, :].astype(jnp.float32), 0.0)
            out_ref[:, low:high, :] += weight * made.reshape(X, high - low, Z)
        return carry

    lax.fori_loop(0, live_ref[0], one_slot, 0)


def blur(live, cells, bands, weights, cell_slot):
    a1, a2, a2b, bz = bands
    vmem = pl.BlockSpec(memory_space=pltpu.VMEM)
    mask = same_lane()
    return pl.pallas_call(
        blur_kernel,
        out_shape=jax.ShapeDtypeStruct((X, Y, Z), jnp.float32),
        in_specs=[pl.BlockSpec(memory_space=pltpu.SMEM)] + [vmem] * 13,
        out_specs=vmem,
        scratch_shapes=[
            pltpu.VMEM((R, EXT * XO, LANES), jnp.bfloat16),
            pltpu.VMEM((1600, 1536), jnp.bfloat16),
            pltpu.VMEM((2, Y * XO, EXT * XO), jnp.bfloat16),
        ],
        compiler_params=pltpu.CompilerParams(vmem_limit_bytes=60 * 1024 * 1024),
    )(live, *cells, a1, a2, a2b, mask, bz, weights, cell_slot)


def gathered(rows, axis):
    count = lax.axis_size(axis)
    position = lax.axis_index(axis)
    bit = 1
    while bit < count:
        other = lax.ppermute(rows, axis, [(i, i ^ bit) for i in range(count)])
        upper = (position & bit) != 0
        rows = jnp.concatenate(
            [jnp.where(upper, other, rows), jnp.where(upper, rows, other)], axis=0
        )
        bit *= 2
    return rows


def both_ways(to_next, to_last, axis):
    count = lax.axis_size(axis)
    ends = count - 1
    return (
        lax.ppermute(to_next, axis, [(i, (i + 1) % count) for i in range(ends)]),
        lax.ppermute(to_last, axis, [((i + 1) % count, i) for i in range(ends)]),
    )


def lane_part():
    return lax.broadcasted_iota(jnp.int32, (1, NARROW), 1) // HALF


def cut_kernel(reflect_ref, own_ref, next_ref, last_ref, deeper_ref, shallower_ref):
    part = lane_part()
    for g in range(Y // 8):
        rows = [reflect_ref[:, 8 * g + k, :] for k in range(8)]
        for pair in range(4):
            two = rows[2 * pair : 2 * pair + 2]
            own_ref[4 * g + pair] = jnp.concatenate(two, axis=0).astype(jnp.bfloat16)
            next_ref[4 * g + pair] = jnp.concatenate([v[X - HALF :] for v in two], axis=0).astype(jnp.bfloat16)
            last_ref[4 * g + pair] = jnp.concatenate([v[:HALF] for v in two], axis=0).astype(jnp.bfloat16)
        for ref, first in ((deeper_ref, Z - HALF), (shallower_ref, 0)):
            packed = []
            for s in range(2):
                value = None
                for k in range(4):
                    shift = (k * HALF - first) % NARROW
                    turned = rows[2 * k + s]
                    turned = pltpu.roll(turned, shift, 1) if shift else turned
                    value = turned if value is None else jnp.where(part == k, turned, value)
                packed.append(value)
            ref[g] = jnp.concatenate(packed, axis=0).astype(jnp.bfloat16)


def cut(reflect):
    shapes = [(20, 80, Z), (20, 64, Z), (20, 64, Z), (5, 80, NARROW), (5, 80, NARROW)]
    vmem = pl.BlockSpec(memory_space=pltpu.VMEM)
    return pl.pallas_call(
        cut_kernel,
        out_shape=[jax.ShapeDtypeStruct(shape, jnp.bfloat16) for shape in shapes],
        in_specs=[vmem],
        out_specs=[vmem] * 5,
    )(reflect)


def tail_kernel(left_ref, right_ref, after_ref, own_ref, next_ref, last_ref):
    part = lane_part()
    for g in range(5):
        left = left_ref[g].astype(jnp.float32)
        right = right_ref[g].astype(jnp.float32)
        for a in range(2):
            value = left if a == 0 else pltpu.roll(left, 64, 1)
            for k, (source, at) in enumerate(((right, 2 * a), (left, 2 * a + 1), (right, 2 * a + 1)), 1):
                shift = ((k - at) * HALF) % NARROW
                turned = pltpu.roll(source, shift, 1) if shift else source
                value = jnp.where(part == k, turned, value)
            own_ref[2 * g + a] = value.astype(jnp.bfloat16)
            next_ref[2 * g + a] = jnp.concatenate(
                [value[X - HALF : X], value[2 * X - HALF :]], axis=0
            ).astype(jnp.bfloat16)
            last_ref[2 * g + a] = jnp.concatenate(
                [value[:HALF], value[X : X + HALF]], axis=0
            ).astype(jnp.bfloat16)


def unpack_tail(left, right, after):
    shapes = [(10, 80, NARROW), (10, 64, NARROW), (10, 64, NARROW)]
    vmem = pl.BlockSpec(memory_space=pltpu.VMEM)
    return pl.pallas_call(
        tail_kernel,
        out_shape=[jax.ShapeDtypeStruct(shape, jnp.bfloat16) for shape in shapes],
        in_specs=[vmem, vmem, pl.BlockSpec(memory_space=pl.ANY)],
        out_specs=[vmem] * 3,
    )(left, right, after)


def join_kernel(before_ref, own_ref, after_ref, all_ref, next_ref, last_ref):
    count = own_ref.shape[0]
    edge = next_ref.shape[0]
    for ref, start in ((all_ref, 0), (next_ref, count - edge), (last_ref, 0)):
        rows = slice(start, start + ref.shape[0])
        ref[:, 0:64, :] = before_ref[rows]
        ref[:, 64:144, :] = own_ref[rows]
        ref[:, 144:208, :] = after_ref[rows]


def join(before, own, after):
    count = own.shape[0]
    counts = (count, count * 4 // 5, count * 4 // 5)
    vmem = pl.BlockSpec(memory_space=pltpu.VMEM)
    return pl.pallas_call(
        join_kernel,
        out_shape=[jax.ShapeDtypeStruct((n, ROWS, NARROW), jnp.bfloat16) for n in counts],
        in_specs=[vmem] * 3,
        out_specs=[vmem] * 3,
        compiler_params=pltpu.CompilerParams(vmem_limit_bytes=32 * 1024 * 1024),
    )(before, own, after)


def halo(reflect):
    own, to_next, to_last, deeper, shallower = cut(reflect)
    above, below = both_ways(deeper, shallower, "gz")
    before, after = both_ways(to_next, to_last, "il")
    main, to_next, to_last = join(before, own, after)
    left, right = both_ways(to_next, to_last, "xl")
    tail, to_next, to_last = unpack_tail(above, below, main)
    before, after = both_ways(to_next, to_last, "il")
    tail, to_next, to_last = join(before, tail, after)
    left_tail, right_tail = both_ways(to_next, to_last, "xl")
    return left, main, right, left_tail, tail, right_tail


def per_device(reflect, weights, cell_slot, factors, reader_list):
    listed = reader_list.reshape(NEED)
    live_count = jnp.sum((listed >= 0).astype(jnp.int32))
    bands = make_bands(listed, gathered(factors, "xl"))
    return blur(live_count.reshape(1), halo(reflect), bands, weights, cell_slot)


def solution(mesh):
    in_specs = (
        P("il", "xl", "gz"),
        P(None, "il", "xl", "gz"),
        P(None, "il", "xl", "gz"),
        P(("il", "xl", "gz"), None),
        P("il", "xl", "gz", None),
    )
    out_specs = P("il", "xl", "gz")
    return jax.shard_map(
        per_device, mesh=mesh, in_specs=in_specs, out_specs=out_specs, check_vma=False
    )
```

```python
import jax
import jax.numpy as jnp
import numpy as np
from jax import lax
from jax.experimental import pallas as pl
from jax.experimental.pallas import tpu as pltpu
from jax.sharding import PartitionSpec as P

K = 64
R = 8
CP_DEV = 4
NEED = 3
HALF = 32
X, Y, Z = 40, 40, 128
XO = 4
XB = X // XO
LANES = XB * 192
EXT = 104
ROWS = 2 * EXT
NARROW = 128
TOP = 32


def same_lane():
    return jnp.asarray(np.arange(EXT * XO)[None, :] % XO == np.arange(XO)[:, None], jnp.bfloat16)


def tap_maps():
    reverse = np.zeros((128, 128), np.float32)
    repeat = np.zeros((128, 256), np.float32)
    for t in range(K):
        reverse[t, -t % 128] = 1
        repeat[t, XO * t : XO * (t + 1)] = 1
    return jnp.asarray(np.concatenate([reverse, repeat], axis=1), jnp.bfloat16)


def bands_kernel(list_ref, table_ref, map_ref, a1_ref, a2_ref, a2b_ref, bz_ref, table, taps, long):
    for tile in range(12):
        table[tile] = table_ref[:, tile * 128 : (tile + 1) * 128].astype(jnp.float32)
    lane = lax.broadcasted_iota(jnp.int32, (1, 128), 1)
    for slot in range(NEED):
        listed = jnp.maximum(list_ref[slot], 0)
        key = (listed // (CP_DEV * 8)) % 8 * CP_DEV + listed % CP_DEV
        for r in range(R):
            for axis in range(3):
                tile, half = divmod(3 * r + axis, 2)
                piece = table[tile, pl.ds(key, 1), :]
                if half:
                    piece = pltpu.roll(piece, 64, 1)
                at = axis * NEED * R + slot * R + r
                taps[at : at + 1, :] = jnp.where(lane < K, piece, 0.0)
    mapped = jnp.dot(
        taps[...].astype(jnp.bfloat16), map_ref[...], preferred_element_type=jnp.float32
    )
    for tile in range(3):
        long[tile] = mapped[:, tile * 128 : (tile + 1) * 128]

    row8 = lax.broadcasted_iota(jnp.int32, (8, 128), 0)
    lane8 = lax.broadcasted_iota(jnp.int32, (8, 128), 1)
    low = row8 < 4

    def between(first, last):
        return (lane8 >= first) & (lane8 < last)

    plain = low & between(0, 32)
    by_32 = (low & between(64, 104)) | (~low & between(32, 64))
    by_72 = ~low & between(104, 128)
    end_72 = (low & between(16, 48)) | (~low & between(0, 16))
    end_104 = ~low & between(48, 80)
    row_z = lax.broadcasted_iota(jnp.int32, (128, 128), 0)
    lane_z = lax.broadcasted_iota(jnp.int32, (128, 128), 1)
    inside = lane_z <= row_z
    row_y = lax.broadcasted_iota(jnp.int32, (TOP, 128), 0)
    lane_y = lax.broadcasted_iota(jnp.int32, (TOP, 128), 1)
    after = lane_y >= XO * row_y
    after8 = lane8 >= XO * row8

    def one_term(i, carry):
        slot = i // R
        r = i % R
        row = jnp.broadcast_to(taps[pl.ds(i, 1), :], (8, 128))
        base = pltpu.roll(row, 0, 1, stride=1, stride_axis=0)
        base = jnp.where(low, base, pltpu.roll(base, 124, 1))
        for b in range(0, XB, 2):
            ends = ([], [])
            for c in (b, b + 1):
                turned = [
                    pltpu.roll(base, (XO * c + k) % 128, 1) if (XO * c + k) % 128 else base
                    for k in (0, 32, 72, 104)
                ]
                ends[0].append(
                    jnp.where(plain, turned[0], jnp.where(by_32, turned[1], jnp.where(by_72, turned[2], 0.0)))
                )
                ends[1].append(jnp.where(end_72, turned[2], jnp.where(end_104, turned[3], 0.0)))
            rows = pl.ds(pl.multiple_of(r * (XB * 8) + b * 8, 16), 16)
            a1_ref[slot, rows, 0:128] = jnp.concatenate(ends[0], axis=0).astype(jnp.bfloat16)
            a1_ref[slot, rows, 128:ROWS] = jnp.concatenate(ends[1], axis=0)[:, : ROWS - 128].astype(jnp.bfloat16)
        halves = [
            pltpu.roll(
                jnp.broadcast_to(long[k, pl.ds(NEED * R + i, 1), :], (TOP, 128)),
                0, 1, stride=XO, stride_axis=0,
            )
            for k in (1, 2)
        ]
        zero = jnp.zeros((TOP, 128), jnp.float32)
        tiles = [
            jnp.where(after, halves[0], 0.0),
            jnp.where(after, halves[1], halves[0]),
            jnp.where(after, 0.0, halves[1]),
            zero,
        ]
        for k in range(4):
            width = min(128, EXT * XO - 128 * k)
            a2_ref[i, :, 128 * k : 128 * k + width] = tiles[k][:, :width].astype(jnp.bfloat16)
        ends = [
            jnp.zeros((8, 128), jnp.float32),
            jnp.where(after8, halves[0][:8], 0.0),
            jnp.where(after8, halves[1][:8], halves[0][:8]),
            jnp.where(after8, 0.0, halves[1][:8]),
        ]
        for k in range(4):
            width = min(128, EXT * XO - 128 * k)
            for o in range(0, XO, 2):
                two = jnp.concatenate(
                    [jnp.where(lane8 % XO == c, ends[k], 0.0) for c in (o, o + 1)], axis=0
                )
                a2b_ref[i, 8 * o : 8 * o + 16, 128 * k : 128 * k + width] = two[:, :width].astype(jnp.bfloat16)
        row = jnp.broadcast_to(long[0, pl.ds(2 * NEED * R + i, 1), :], (128, 128))
        turned = pltpu.roll(row, 0, 1, stride=1, stride_axis=0)
        first = jnp.where(inside, turned, 0.0).astype(jnp.bfloat16)
        second = jnp.where(inside, 0.0, turned).astype(jnp.bfloat16)
        start = (r // 2) * (2 * (Z + 2 * HALF))
        own = pl.multiple_of(start + (r % 2) * Z, 128)
        bz_ref[slot, pl.ds(own, 96), :] = first[32:]
        bz_ref[slot, pl.ds(own + 96, 32), :] = second[:32]
        ends = pl.multiple_of(start + 2 * Z + (r % 2) * 2 * HALF, 64)
        bz_ref[slot, pl.ds(ends, 32), :] = first[:32]
        bz_ref[slot, pl.ds(ends + 32, 32), :] = second[32:64]
        return carry

    lax.fori_loop(0, NEED * R, one_term, 0)


def make_bands(listed, table):
    shapes = [
        (NEED, R * XB * 8, ROWS),
        (NEED * R, TOP, EXT * XO),
        (NEED * R, XO * (Y - TOP), EXT * XO),
        (NEED, R * (Z + 2 * HALF), Z),
    ]
    vmem = pl.BlockSpec(memory_space=pltpu.VMEM)
    return pl.pallas_call(
        bands_kernel,
        out_shape=[jax.ShapeDtypeStruct(shape, jnp.bfloat16) for shape in shapes],
        in_specs=[pl.BlockSpec(memory_space=pltpu.SMEM), vmem, vmem],
        out_specs=[vmem] * 4,
        scratch_shapes=[
            pltpu.VMEM((12, 32, 128), jnp.float32),
            pltpu.VMEM((3 * NEED * R, 128), jnp.float32),
            pltpu.VMEM((3, 3 * NEED * R, 128), jnp.float32),
        ],
        compiler_params=pltpu.CompilerParams(vmem_limit_bytes=32 * 1024 * 1024),
    )(listed, table, tap_maps())


def roll_half(value):
    return pltpu.roll(value, 64, 1)


def blur_kernel(
    live_ref, left_ref, own_ref, right_ref, a1_ref, a2_ref, a2b_ref, mask_ref, bz_ref,
    weights_ref, slot_ref, out_ref, line_x, line_y, band_y,
):
    out_ref[...] = jnp.zeros_like(out_ref)
    low_x = lax.broadcasted_iota(jnp.int32, (8, NARROW), 1) < 64
    low_y = lax.broadcasted_iota(jnp.int32, (TOP * XO, NARROW), 1) < 64
    low_b = lax.broadcasted_iota(jnp.int32, ((Y - TOP) * XO, NARROW), 1) < 64

    def one_slot(slot, carry):
        def stage_x(part, offset):
            pairs = part.shape[0] * 2 // 3

            def step(i, carry):
                g = 2 * i
                rhs = jnp.concatenate(
                    [part[4 * i], part[4 * i + 1], part[4 * i + 2], part[4 * i + 3], part[pairs + g], part[pairs + g + 1]],
                    axis=1,
                )
                made = jnp.dot(a1_ref[slot], rhs, preferred_element_type=jnp.float32)
                base = pl.multiple_of((offset + g) * 16, 32)

                def cell(r, b, k):
                    row = (r * XB + b) * 8
                    return made[row : row + 8, k * 128 : (k + 1) * 128]

                def put(r, k, column, first, second):
                    line_x[r, pl.ds(base + k * 16, 16), column * 128 : (column + 1) * 128] = (
                        jnp.concatenate([first, second], axis=0).astype(jnp.bfloat16)
                    )

                for r in range(R):
                    for k in range(2):
                        for b in range(XB):
                            put(r, k, b, cell(r, b, 2 * k), cell(r, b, 2 * k + 1))
                        for c in range(XB // 2):
                            one, two = cell(r, 2 * c, 4 + k), cell(r, 2 * c + 1, 4 + k)
                            put(
                                r, k, XB + c,
                                jnp.where(low_x, one, roll_half(two)),
                                jnp.where(low_x, roll_half(one), two),
                            )
                return carry

            lax.fori_loop(0, pairs // 4, step, 0)

        stage_x(left_ref, 0)
        stage_x(own_ref, 8)
        stage_x(right_ref, 18)

        def pair(q, carry):
            made = []
            for h in range(2):
                r = 2 * q + h
                top = a2_ref[slot * R + r]
                for o in range(XO):
                    band_y[h, o * TOP : (o + 1) * TOP, :] = top * mask_ref[o : o + 1, :]
                band_y[h, TOP * XO :, :] = a2b_ref[slot * R + r]
                made.append(jnp.dot(band_y[h], line_x[r], preferred_element_type=jnp.float32))
            lanes = pl.multiple_of(q * 384, 128)
            tail = pl.ds(lanes + 256, 128)
            for first, count, start, low in ((0, TOP * XO, 0, low_y), (TOP * XO, (Y - TOP) * XO, TOP * X, low_b)):

                def cell(h, column):
                    return made[h][first : first + count, column * 128 : (column + 1) * 128]

                def rows(b):
                    return slice(start + b * count, start + (b + 1) * count)

                for b in range(XB):
                    for h in range(2):
                        line_y[rows(b), pl.ds(lanes + h * 128, 128)] = cell(h, b).astype(jnp.bfloat16)
                for c in range(XB // 2):
                    one, two = cell(0, XB + c), cell(1, XB + c)
                    line_y[rows(2 * c), tail] = jnp.where(low, one, roll_half(two)).astype(jnp.bfloat16)
                    line_y[rows(2 * c + 1), tail] = jnp.where(low, roll_half(one), two).astype(jnp.bfloat16)
            return carry

        lax.fori_loop(0, R // 2, pair, 0)

        done = jnp.dot(line_y[...], bz_ref[slot], preferred_element_type=jnp.float32)
        for low, high, made in ((0, TOP, done[:1280]), (TOP, Y, done[1280:])):
            weight = jnp.zeros((X, high - low, Z), jnp.float32)
            for j in range(2):
                here = slot_ref[j, :, low:high, :] == slot
                weight = weight + jnp.where(here, weights_ref[j, :, low:high, :].astype(jnp.float32), 0.0)
            out_ref[:, low:high, :] += weight * made.reshape(X, high - low, Z)
        return carry

    lax.fori_loop(0, live_ref[0], one_slot, 0)


def blur(live, cells, bands, weights, cell_slot):
    a1, a2, a2b, bz = bands
    vmem = pl.BlockSpec(memory_space=pltpu.VMEM)
    mask = same_lane()
    return pl.pallas_call(
        blur_kernel,
        out_shape=jax.ShapeDtypeStruct((X, Y, Z), jnp.float32),
        in_specs=[pl.BlockSpec(memory_space=pltpu.SMEM)] + [vmem] * 10,
        out_specs=vmem,
        scratch_shapes=[
            pltpu.VMEM((R, EXT * XO, LANES), jnp.bfloat16),
            pltpu.VMEM((1600, 1536), jnp.bfloat16),
            pltpu.VMEM((2, Y * XO, EXT * XO), jnp.bfloat16),
        ],
        compiler_params=pltpu.CompilerParams(vmem_limit_bytes=40 * 1024 * 1024),
    )(live, *cells, a1, a2, a2b, mask, bz, weights, cell_slot)


def gathered(rows, axis):
    count = lax.axis_size(axis)
    position = lax.axis_index(axis)
    bit = 1
    while bit < count:
        other = lax.ppermute(rows, axis, [(i, i ^ bit) for i in range(count)])
        upper = (position & bit) != 0
        rows = jnp.concatenate(
            [jnp.where(upper, other, rows), jnp.where(upper, rows, other)], axis=0
        )
        bit *= 2
    return rows


def both_ways(to_next, to_last, axis):
    count = lax.axis_size(axis)
    ends = count - 1
    after = lax.ppermute(to_last, axis, [((i + 1) % count, i) for i in range(ends)])
    before = lax.ppermute(to_next, axis, [(i, (i + 1) % count) for i in range(ends)])
    return before, after


def lane_part():
    return lax.broadcasted_iota(jnp.int32, (1, NARROW), 1) // HALF


def cut_kernel(reflect_ref, own_ref, next_ref, last_ref, deeper_ref, shallower_ref):
    part = lane_part()
    for g in range(Y // 8):
        rows = [reflect_ref[:, 8 * g + k, :] for k in range(8)]
        for pair in range(4):
            two = rows[2 * pair : 2 * pair + 2]
            own_ref[4 * g + pair] = jnp.concatenate(two, axis=0).astype(jnp.bfloat16)
            next_ref[4 * g + pair] = jnp.concatenate([v[X - HALF :] for v in two], axis=0).astype(jnp.bfloat16)
            last_ref[4 * g + pair] = jnp.concatenate([v[:HALF] for v in two], axis=0).astype(jnp.bfloat16)
        for ref, first in ((deeper_ref, Z - HALF), (shallower_ref, 0)):
            packed = []
            for s in range(2):
                value = None
                for k in range(4):
                    shift = (k * HALF - first) % NARROW
                    turned = rows[2 * k + s]
                    turned = pltpu.roll(turned, shift, 1) if shift else turned
                    value = turned if value is None else jnp.where(part == k, turned, value)
                packed.append(value)
            ref[g] = jnp.concatenate(packed, axis=0).astype(jnp.bfloat16)


def cut(reflect):
    shapes = [(20, 80, Z), (20, 64, Z), (20, 64, Z), (5, 80, NARROW), (5, 80, NARROW)]
    vmem = pl.BlockSpec(memory_space=pltpu.VMEM)
    return pl.pallas_call(
        cut_kernel,
        out_shape=[jax.ShapeDtypeStruct(shape, jnp.bfloat16) for shape in shapes],
        in_specs=[vmem],
        out_specs=[vmem] * 5,
    )(reflect)


def tail_kernel(left_ref, right_ref, main_next, main_last, own_ref, next_ref, last_ref):
    part = lane_part()
    next_ref[:20] = main_next[...]
    last_ref[:20] = main_last[...]
    for g in range(5):
        left = left_ref[g].astype(jnp.float32)
        right = right_ref[g].astype(jnp.float32)
        for a in range(2):
            value = left if a == 0 else pltpu.roll(left, 64, 1)
            for k, (source, at) in enumerate(((right, 2 * a), (left, 2 * a + 1), (right, 2 * a + 1)), 1):
                shift = ((k - at) * HALF) % NARROW
                turned = pltpu.roll(source, shift, 1) if shift else source
                value = jnp.where(part == k, turned, value)
            own_ref[2 * g + a] = value.astype(jnp.bfloat16)
            next_ref[20 + 2 * g + a] = jnp.concatenate(
                [value[X - HALF : X], value[2 * X - HALF :]], axis=0
            ).astype(jnp.bfloat16)
            last_ref[20 + 2 * g + a] = jnp.concatenate(
                [value[:HALF], value[X : X + HALF]], axis=0
            ).astype(jnp.bfloat16)


def unpack_tail(left, right, main_next, main_last):
    shapes = [(10, 80, NARROW), (30, 64, NARROW), (30, 64, NARROW)]
    vmem = pl.BlockSpec(memory_space=pltpu.VMEM)
    return pl.pallas_call(
        tail_kernel,
        out_shape=[jax.ShapeDtypeStruct(shape, jnp.bfloat16) for shape in shapes],
        in_specs=[vmem] * 4,
        out_specs=[vmem] * 3,
    )(left, right, main_next, main_last)


def join_kernel(before_ref, own_ref, tail_ref, after_ref, all_ref, next_ref, last_ref):
    for ref, to, at, count in (
        (all_ref, 0, 0, 30),
        (next_ref, 0, 4, 16),
        (next_ref, 16, 22, 8),
        (last_ref, 0, 0, 16),
        (last_ref, 16, 20, 8),
    ):
        ref[to : to + count, 0:64, :] = before_ref[at : at + count]
        ref[to : to + count, 144:208, :] = after_ref[at : at + count]
        mains = min(max(20 - at, 0), count)
        if mains:
            ref[to : to + mains, 64:144, :] = own_ref[at : at + mains]
        if count > mains:
            first = max(at - 20, 0)
            ref[to + mains : to + count, 64:144, :] = tail_ref[first : first + count - mains]


def join(before, own, tail, after):
    vmem = pl.BlockSpec(memory_space=pltpu.VMEM)
    return pl.pallas_call(
        join_kernel,
        out_shape=[jax.ShapeDtypeStruct((n, ROWS, NARROW), jnp.bfloat16) for n in (30, 24, 24)],
        in_specs=[vmem] * 4,
        out_specs=[vmem] * 3,
        compiler_params=pltpu.CompilerParams(vmem_limit_bytes=24 * 1024 * 1024),
    )(before, own, tail, after)


def halo(reflect):
    own, to_next, to_last, deeper, shallower = cut(reflect)
    above, below = both_ways(deeper, shallower, "gz")
    tail, to_next, to_last = unpack_tail(above, below, to_next, to_last)
    before, after = both_ways(to_next, to_last, "il")
    block, to_next, to_last = join(before, own, tail, after)
    left, right = both_ways(to_next, to_last, "xl")
    return left, block, right


def per_device(reflect, weights, cell_slot, factors, reader_list):
    listed = reader_list.reshape(NEED)
    live_count = jnp.sum((listed >= 0).astype(jnp.int32))
    bands = make_bands(listed, gathered(factors, "xl"))
    return blur(live_count.reshape(1), halo(reflect), bands, weights, cell_slot)


def solution(mesh):
    in_specs = (
        P("il", "xl", "gz"),
        P(None, "il", "xl", "gz"),
        P(None, "il", "xl", "gz"),
        P(("il", "xl", "gz"), None),
        P("il", "xl", "gz", None),
    )
    out_specs = P("il", "xl", "gz")
    return jax.shard_map(
        per_device, mesh=mesh, in_specs=in_specs, out_specs=out_specs, check_vma=False
    )
```

```python
import jax
import jax.numpy as jnp
import numpy as np
from jax import lax
from jax.experimental import pallas as pl
from jax.experimental.pallas import tpu as pltpu
from jax.sharding import PartitionSpec as P

K = 64
R = 8
CP_DEV = 4
NEED = 3
HALF = 32
X, Y, Z = 40, 40, 128
XO = 4
XB = X // XO
LANES = XB * 192
OWN_LIMIT = 24 * 1024 * 1024
BLUR_LIMIT = 22 * 1024 * 1024
EXT = 104
ROWS = 2 * EXT
NARROW = 128
TOP = 32


def same_lane():
    return jnp.asarray(np.arange(EXT * XO)[None, :] % XO == np.arange(XO)[:, None], jnp.bfloat16)


def tap_maps():
    reverse = np.zeros((128, 128), np.float32)
    repeat = np.zeros((128, 256), np.float32)
    for t in range(K):
        reverse[t, -t % 128] = 1
        repeat[t, XO * t : XO * (t + 1)] = 1
    return jnp.asarray(np.concatenate([reverse, repeat], axis=1), jnp.bfloat16)


def bands_kernel(list_ref, table_ref, map_ref, a1_ref, a2_ref, a2b_ref, bz_ref, table, taps, long):
    for tile in range(12):
        table[tile] = table_ref[:, tile * 128 : (tile + 1) * 128].astype(jnp.float32)
    lane = lax.broadcasted_iota(jnp.int32, (1, 128), 1)
    for slot in range(NEED):
        listed = jnp.maximum(list_ref[slot], 0)
        key = (listed // (CP_DEV * 8)) % 8 * CP_DEV + listed % CP_DEV
        for r in range(R):
            for axis in range(3):
                tile, half = divmod(3 * r + axis, 2)
                piece = table[tile, pl.ds(key, 1), :]
                if half:
                    piece = pltpu.roll(piece, 64, 1)
                at = axis * NEED * R + slot * R + r
                taps[at : at + 1, :] = jnp.where(lane < K, piece, 0.0)
    mapped = jnp.dot(
        taps[...].astype(jnp.bfloat16), map_ref[...], preferred_element_type=jnp.float32
    )
    for tile in range(3):
        long[tile] = mapped[:, tile * 128 : (tile + 1) * 128]

    row8 = lax.broadcasted_iota(jnp.int32, (8, 128), 0)
    lane8 = lax.broadcasted_iota(jnp.int32, (8, 128), 1)
    low = row8 < 4

    def between(first, last):
        return (lane8 >= first) & (lane8 < last)

    plain = low & between(0, 32)
    by_32 = (low & between(64, 104)) | (~low & between(32, 64))
    by_72 = ~low & between(104, 128)
    end_72 = (low & between(16, 48)) | (~low & between(0, 16))
    end_104 = ~low & between(48, 80)
    row_z = lax.broadcasted_iota(jnp.int32, (128, 128), 0)
    lane_z = lax.broadcasted_iota(jnp.int32, (128, 128), 1)
    inside = lane_z <= row_z
    row_y = lax.broadcasted_iota(jnp.int32, (TOP, 128), 0)
    lane_y = lax.broadcasted_iota(jnp.int32, (TOP, 128), 1)
    after = lane_y >= XO * row_y
    after8 = lane8 >= XO * row8

    def one_term(i, carry):
        slot = i // R
        r = i % R
        row = jnp.broadcast_to(taps[pl.ds(i, 1), :], (8, 128))
        base = pltpu.roll(row, 0, 1, stride=1, stride_axis=0)
        base = jnp.where(low, base, pltpu.roll(base, 124, 1))
        for b in range(0, XB, 2):
            ends = ([], [])
            for c in (b, b + 1):
                turned = [
                    pltpu.roll(base, (XO * c + k) % 128, 1) if (XO * c + k) % 128 else base
                    for k in (0, 32, 72, 104)
                ]
                ends[0].append(
                    jnp.where(plain, turned[0], jnp.where(by_32, turned[1], jnp.where(by_72, turned[2], 0.0)))
                )
                ends[1].append(jnp.where(end_72, turned[2], jnp.where(end_104, turned[3], 0.0)))
            rows = pl.ds(pl.multiple_of(r * (XB * 8) + b * 8, 16), 16)
            a1_ref[slot, rows, 0:128] = jnp.concatenate(ends[0], axis=0).astype(jnp.bfloat16)
            a1_ref[slot, rows, 128:ROWS] = jnp.concatenate(ends[1], axis=0)[:, : ROWS - 128].astype(jnp.bfloat16)
        halves = [
            pltpu.roll(
                jnp.broadcast_to(long[k, pl.ds(NEED * R + i, 1), :], (TOP, 128)),
                0, 1, stride=XO, stride_axis=0,
            )
            for k in (1, 2)
        ]
        zero = jnp.zeros((TOP, 128), jnp.float32)
        tiles = [
            jnp.where(after, halves[0], 0.0),
            jnp.where(after, halves[1], halves[0]),
            jnp.where(after, 0.0, halves[1]),
            zero,
        ]
        for k in range(4):
            width = min(128, EXT * XO - 128 * k)
            a2_ref[i, :, 128 * k : 128 * k + width] = tiles[k][:, :width].astype(jnp.bfloat16)
        ends = [
            jnp.zeros((8, 128), jnp.float32),
            jnp.where(after8, halves[0][:8], 0.0),
            jnp.where(after8, halves[1][:8], halves[0][:8]),
            jnp.where(after8, 0.0, halves[1][:8]),
        ]
        for k in range(4):
            width = min(128, EXT * XO - 128 * k)
            for o in range(0, XO, 2):
                two = jnp.concatenate(
                    [jnp.where(lane8 % XO == c, ends[k], 0.0) for c in (o, o + 1)], axis=0
                )
                a2b_ref[i, 8 * o : 8 * o + 16, 128 * k : 128 * k + width] = two[:, :width].astype(jnp.bfloat16)
        row = jnp.broadcast_to(long[0, pl.ds(2 * NEED * R + i, 1), :], (128, 128))
        turned = pltpu.roll(row, 0, 1, stride=1, stride_axis=0)
        first = jnp.where(inside, turned, 0.0).astype(jnp.bfloat16)
        second = jnp.where(inside, 0.0, turned).astype(jnp.bfloat16)
        start = (r // 2) * (2 * (Z + 2 * HALF))
        own = pl.multiple_of(start + (r % 2) * Z, 128)
        bz_ref[slot, pl.ds(own, 96), :] = first[32:]
        bz_ref[slot, pl.ds(own + 96, 32), :] = second[:32]
        ends = pl.multiple_of(start + 2 * Z + (r % 2) * 2 * HALF, 64)
        bz_ref[slot, pl.ds(ends, 32), :] = first[:32]
        bz_ref[slot, pl.ds(ends + 32, 32), :] = second[32:64]
        return carry

    lax.fori_loop(0, NEED * R, one_term, 0)


def make_bands(listed, table):
    shapes = [
        (NEED, R * XB * 8, ROWS),
        (NEED * R, TOP, EXT * XO),
        (NEED * R, XO * (Y - TOP), EXT * XO),
        (NEED, R * (Z + 2 * HALF), Z),
    ]
    vmem = pl.BlockSpec(memory_space=pltpu.VMEM)
    return pl.pallas_call(
        bands_kernel,
        out_shape=[jax.ShapeDtypeStruct(shape, jnp.bfloat16) for shape in shapes],
        in_specs=[pl.BlockSpec(memory_space=pltpu.SMEM), vmem, vmem],
        out_specs=[vmem] * 4,
        scratch_shapes=[
            pltpu.VMEM((12, 32, 128), jnp.float32),
            pltpu.VMEM((3 * NEED * R, 128), jnp.float32),
            pltpu.VMEM((3, 3 * NEED * R, 128), jnp.float32),
        ],
        compiler_params=pltpu.CompilerParams(vmem_limit_bytes=14 * 1024 * 1024),
    )(listed, table, tap_maps())


def roll_half(value):
    return pltpu.roll(value, 64, 1)


def stage_x(slot, part, a1_ref, put, offset):
    low = lax.broadcasted_iota(jnp.int32, (8, NARROW), 1) < 64
    pairs = part.shape[0] * 2 // 3

    def step(i, carry):
        g = 2 * i
        rhs = jnp.concatenate(
            [part[4 * i], part[4 * i + 1], part[4 * i + 2], part[4 * i + 3], part[pairs + g], part[pairs + g + 1]],
            axis=1,
        )
        made = jnp.dot(a1_ref[slot], rhs, preferred_element_type=jnp.float32)
        base = pl.multiple_of((offset + g) * 16, 32)

        def cell(r, b, k):
            row = (r * XB + b) * 8
            return made[row : row + 8, k * 128 : (k + 1) * 128]

        def place(r, k, column, first, second):
            put(
                r,
                pl.ds(base + k * 16, 16),
                slice(column * 128, (column + 1) * 128),
                jnp.concatenate([first, second], axis=0).astype(jnp.bfloat16),
            )

        for r in range(R):
            for k in range(2):
                for b in range(XB):
                    place(r, k, b, cell(r, b, 2 * k), cell(r, b, 2 * k + 1))
                for c in range(XB // 2):
                    one, two = cell(r, 2 * c, 4 + k), cell(r, 2 * c + 1, 4 + k)
                    place(
                        r, k, XB + c,
                        jnp.where(low, one, roll_half(two)),
                        jnp.where(low, roll_half(one), two),
                    )
        return carry

    lax.fori_loop(0, pairs // 4, step, 0)


def own_kernel(live_ref, own_ref, a1_ref, out_ref):
    def one_slot(slot, carry):
        def put(r, rows, lanes, value):
            out_ref[slot, r, rows, lanes] = value

        stage_x(slot, own_ref, a1_ref, put, 0)
        return carry

    lax.fori_loop(0, live_ref[0], one_slot, 0)


def blur_own(live, own, a1):
    vmem = pl.BlockSpec(memory_space=pltpu.VMEM)
    return pl.pallas_call(
        own_kernel,
        out_shape=jax.ShapeDtypeStruct((NEED, R, Y * XO, LANES), jnp.bfloat16),
        in_specs=[pl.BlockSpec(memory_space=pltpu.SMEM), vmem, vmem],
        out_specs=vmem,
        compiler_params=pltpu.CompilerParams(vmem_limit_bytes=OWN_LIMIT),
        cost_estimate=pl.CostEstimate(flops=8_000_000_000, bytes_accessed=2_000_000, transcendentals=0),
    )(live, own, a1)


def blur_kernel(
    live_ref, left_ref, own_ref, right_ref, a1_ref, a2_ref, a2b_ref, mask_ref, bz_ref,
    weights_ref, slot_ref, out_ref, line_x, line_y, band_y,
):
    out_ref[...] = jnp.zeros_like(out_ref)
    low_y = lax.broadcasted_iota(jnp.int32, (TOP * XO, NARROW), 1) < 64
    low_b = lax.broadcasted_iota(jnp.int32, ((Y - TOP) * XO, NARROW), 1) < 64
    side = HALF * XO

    def one_slot(slot, carry):
        def put(r, rows, lanes, value):
            line_x[r, rows, lanes] = value

        stage_x(slot, left_ref, a1_ref, put, 0)
        stage_x(slot, right_ref, a1_ref, put, 8)

        def pair(q, carry):
            made = []
            for h in range(2):
                r = 2 * q + h
                top = a2_ref[slot * R + r]
                for o in range(XO):
                    band_y[h, o * TOP : (o + 1) * TOP, :] = top * mask_ref[o : o + 1, :]
                band_y[h, TOP * XO :, :] = a2b_ref[slot * R + r]
                lines = jnp.concatenate([line_x[r, :side], own_ref[slot, r], line_x[r, side:]], axis=0)
                made.append(jnp.dot(band_y[h], lines, preferred_element_type=jnp.float32))
            lanes = pl.multiple_of(q * 384, 128)
            tail = pl.ds(lanes + 256, 128)
            for first, count, start, low in ((0, TOP * XO, 0, low_y), (TOP * XO, (Y - TOP) * XO, TOP * X, low_b)):

                def cell(h, column):
                    return made[h][first : first + count, column * 128 : (column + 1) * 128]

                def rows(b):
                    return slice(start + b * count, start + (b + 1) * count)

                for b in range(XB):
                    for h in range(2):
                        line_y[rows(b), pl.ds(lanes + h * 128, 128)] = cell(h, b).astype(jnp.bfloat16)
                for c in range(XB // 2):
                    one, two = cell(0, XB + c), cell(1, XB + c)
                    line_y[rows(2 * c), tail] = jnp.where(low, one, roll_half(two)).astype(jnp.bfloat16)
                    line_y[rows(2 * c + 1), tail] = jnp.where(low, roll_half(one), two).astype(jnp.bfloat16)
            return carry

        lax.fori_loop(0, R // 2, pair, 0)

        done = jnp.dot(line_y[...], bz_ref[slot], preferred_element_type=jnp.float32)
        for low, high, made in ((0, TOP, done[:1280]), (TOP, Y, done[1280:])):
            weight = jnp.zeros((X, high - low, Z), jnp.float32)
            for j in range(2):
                here = slot_ref[j, :, low:high, :] == slot
                weight = weight + jnp.where(here, weights_ref[j, :, low:high, :].astype(jnp.float32), 0.0)
            out_ref[:, low:high, :] += weight * made.reshape(X, high - low, Z)
        return carry

    lax.fori_loop(0, live_ref[0], one_slot, 0)


def blur(live, cells, bands, weights, cell_slot):
    a1, a2, a2b, bz = bands
    left, own, right = cells
    own = blur_own(live, own, a1)
    vmem = pl.BlockSpec(memory_space=pltpu.VMEM)
    mask = same_lane()
    return pl.pallas_call(
        blur_kernel,
        out_shape=jax.ShapeDtypeStruct((X, Y, Z), jnp.float32),
        in_specs=[pl.BlockSpec(memory_space=pltpu.SMEM)] + [vmem] * 10,
        out_specs=vmem,
        scratch_shapes=[
            pltpu.VMEM((R, 2 * HALF * XO, LANES), jnp.bfloat16),
            pltpu.VMEM((1600, 1536), jnp.bfloat16),
            pltpu.VMEM((2, Y * XO, EXT * XO), jnp.bfloat16),
        ],
        compiler_params=pltpu.CompilerParams(vmem_limit_bytes=BLUR_LIMIT),
    )(live, left, own, right, a1, a2, a2b, mask, bz, weights, cell_slot)


def doubled(rows, axis, bit):
    count = lax.axis_size(axis)
    other = lax.ppermute(rows, axis, [(i, i ^ bit) for i in range(count)])
    upper = (lax.axis_index(axis) & bit) != 0
    return jnp.concatenate(
        [jnp.where(upper, other, rows), jnp.where(upper, rows, other)], axis=0
    )


def both_ways(to_next, to_last, axis):
    count = lax.axis_size(axis)
    ends = count - 1
    after = lax.ppermute(to_last, axis, [((i + 1) % count, i) for i in range(ends)])
    before = lax.ppermute(to_next, axis, [(i, (i + 1) % count) for i in range(ends)])
    return before, after


def lane_part():
    return lax.broadcasted_iota(jnp.int32, (1, NARROW), 1) // HALF


def ends_kernel(reflect_ref, shallower_ref, deeper_ref):
    part = lane_part()
    for g in range(Y // 8):
        rows = [reflect_ref[:, 8 * g + k, :] for k in range(8)]
        for ref, first in ((deeper_ref, Z - HALF), (shallower_ref, 0)):
            packed = []
            for s in range(2):
                value = None
                for k in range(4):
                    shift = (k * HALF - first) % NARROW
                    turned = rows[2 * k + s]
                    turned = pltpu.roll(turned, shift, 1) if shift else turned
                    value = turned if value is None else jnp.where(part == k, turned, value)
                packed.append(value)
            ref[g] = jnp.concatenate(packed, axis=0).astype(jnp.bfloat16)


def depth_ends(reflect):
    vmem = pl.BlockSpec(memory_space=pltpu.VMEM)
    return pl.pallas_call(
        ends_kernel,
        out_shape=[jax.ShapeDtypeStruct((5, 80, NARROW), jnp.bfloat16)] * 2,
        in_specs=[vmem],
        out_specs=[vmem] * 2,
    )(reflect)


def cut_kernel(reflect_ref, factors_ref, after_ref, own_ref, next_ref, last_ref, rows_ref):
    rows_ref[...] = factors_ref[...]
    for pair in range(Y // 2):
        two = [reflect_ref[:, 2 * pair + k, :] for k in range(2)]
        own_ref[pair] = jnp.concatenate(two, axis=0).astype(jnp.bfloat16)
        next_ref[pair] = jnp.concatenate([v[X - HALF :] for v in two], axis=0).astype(jnp.bfloat16)
        last_ref[pair] = jnp.concatenate([v[:HALF] for v in two], axis=0).astype(jnp.bfloat16)


def cut(reflect, factors, after):
    shapes = [(20, 80, Z), (20, 64, Z), (20, 64, Z), factors.shape]
    vmem = pl.BlockSpec(memory_space=pltpu.VMEM)
    return pl.pallas_call(
        cut_kernel,
        out_shape=[jax.ShapeDtypeStruct(shape, jnp.bfloat16) for shape in shapes],
        in_specs=[vmem] * 2 + [pl.BlockSpec(memory_space=pl.ANY)],
        out_specs=[vmem] * 4,
    )(reflect, factors, after)


def tail_kernel(left_ref, right_ref, main_next, main_last, own_ref, next_ref, last_ref):
    part = lane_part()
    next_ref[:20] = main_next[...]
    last_ref[:20] = main_last[...]
    for g in range(5):
        left = left_ref[g].astype(jnp.float32)
        right = right_ref[g].astype(jnp.float32)
        for a in range(2):
            value = left if a == 0 else pltpu.roll(left, 64, 1)
            for k, (source, at) in enumerate(((right, 2 * a), (left, 2 * a + 1), (right, 2 * a + 1)), 1):
                shift = ((k - at) * HALF) % NARROW
                turned = pltpu.roll(source, shift, 1) if shift else source
                value = jnp.where(part == k, turned, value)
            own_ref[2 * g + a] = value.astype(jnp.bfloat16)
            next_ref[20 + 2 * g + a] = jnp.concatenate(
                [value[X - HALF : X], value[2 * X - HALF :]], axis=0
            ).astype(jnp.bfloat16)
            last_ref[20 + 2 * g + a] = jnp.concatenate(
                [value[:HALF], value[X : X + HALF]], axis=0
            ).astype(jnp.bfloat16)


def unpack_tail(left, right, main_next, main_last):
    shapes = [(10, 80, NARROW), (30, 64, NARROW), (30, 64, NARROW)]
    vmem = pl.BlockSpec(memory_space=pltpu.VMEM)
    return pl.pallas_call(
        tail_kernel,
        out_shape=[jax.ShapeDtypeStruct(shape, jnp.bfloat16) for shape in shapes],
        in_specs=[vmem] * 4,
        out_specs=[vmem] * 3,
    )(left, right, main_next, main_last)


def join_kernel(before_ref, own_ref, tail_ref, after_ref, rows_ref, all_ref, next_ref, last_ref):
    for ref, to, at, count in (
        (all_ref, 0, 0, 30),
        (next_ref, 0, 4, 16),
        (next_ref, 16, 22, 8),
        (last_ref, 0, 0, 16),
        (last_ref, 16, 20, 8),
    ):
        ref[to : to + count, 0:64, :] = before_ref[at : at + count]
        ref[to : to + count, 144:208, :] = after_ref[at : at + count]
        mains = min(max(20 - at, 0), count)
        if mains:
            ref[to : to + mains, 64:144, :] = own_ref[at : at + mains]
        if count > mains:
            first = max(at - 20, 0)
            ref[to + mains : to + count, 64:144, :] = tail_ref[first : first + count - mains]


def join(before, own, tail, after, rows):
    vmem = pl.BlockSpec(memory_space=pltpu.VMEM)
    return pl.pallas_call(
        join_kernel,
        out_shape=[jax.ShapeDtypeStruct((n, ROWS, NARROW), jnp.bfloat16) for n in (30, 24, 24)],
        in_specs=[vmem] * 4 + [pl.BlockSpec(memory_space=pl.ANY)],
        out_specs=[vmem] * 3,
        compiler_params=pltpu.CompilerParams(vmem_limit_bytes=12 * 1024 * 1024),
    )(before, own, tail, after, rows)


def exchange(reflect, factors):
    shallower, deeper = depth_ends(reflect)
    above, below = both_ways(deeper, shallower, "gz")
    own, to_next, to_last, rows = cut(reflect, factors, shallower)
    rows = doubled(doubled(rows, "xl", 1), "xl", 2)
    tail, to_next, to_last = unpack_tail(above, below, to_next, to_last)
    before, after = both_ways(to_next, to_last, "il")
    block, to_next, to_last = join(before, own, tail, after, rows)
    rows = doubled(rows, "xl", 4)
    left, right = both_ways(to_next, to_last, "xl")
    return (left, block, right), rows


def per_device(reflect, weights, cell_slot, factors, reader_list):
    listed = reader_list.reshape(NEED)
    live_count = jnp.sum((listed >= 0).astype(jnp.int32))
    cells, rows = exchange(reflect, factors)
    bands = make_bands(listed, rows)
    return blur(live_count.reshape(1), cells, bands, weights, cell_slot)


def solution(mesh):
    in_specs = (
        P("il", "xl", "gz"),
        P(None, "il", "xl", "gz"),
        P(None, "il", "xl", "gz"),
        P(("il", "xl", "gz"), None),
        P("il", "xl", "gz", None),
    )
    out_specs = P("il", "xl", "gz")
    return jax.shard_map(
        per_device, mesh=mesh, in_specs=in_specs, out_specs=out_specs, check_vma=False
    )
```

```python
import jax
import jax.numpy as jnp
import numpy as np
from jax import lax
from jax.experimental import pallas as pl
from jax.experimental.pallas import tpu as pltpu
from jax.sharding import PartitionSpec as P

K = 64
R = 8
CP_DEV = 4
NEED = 3
HALF = 32
X, Y, Z = 40, 40, 128
XO = 4
XB = X // XO
LANES = XB * 192
SMALL_LIMIT = 10 * 1024 * 1024
OWN_LIMIT = 24 * 1024 * 1024
BLUR_LIMIT = 22 * 1024 * 1024
EXT = 104
ROWS = 2 * EXT
NARROW = 128
TOP = 32


def same_lane():
    return jnp.asarray(np.arange(EXT * XO)[None, :] % XO == np.arange(XO)[:, None], jnp.bfloat16)


def tap_maps():
    reverse = np.zeros((128, 128), np.float32)
    repeat = np.zeros((128, 256), np.float32)
    for t in range(K):
        reverse[t, -t % 128] = 1
        repeat[t, XO * t : XO * (t + 1)] = 1
    return jnp.asarray(np.concatenate([reverse, repeat], axis=1), jnp.bfloat16)


def bands_kernel(list_ref, table_ref, map_ref, a1_ref, a2_ref, a2b_ref, bz_ref, table, taps, long):
    for tile in range(12):
        table[tile] = table_ref[:, tile * 128 : (tile + 1) * 128].astype(jnp.float32)
    lane = lax.broadcasted_iota(jnp.int32, (1, 128), 1)
    for slot in range(NEED):
        listed = jnp.maximum(list_ref[slot], 0)
        key = (listed // (CP_DEV * 8)) % 8 * CP_DEV + listed % CP_DEV
        for r in range(R):
            for axis in range(3):
                tile, half = divmod(3 * r + axis, 2)
                piece = table[tile, pl.ds(key, 1), :]
                if half:
                    piece = pltpu.roll(piece, 64, 1)
                at = axis * NEED * R + slot * R + r
                taps[at : at + 1, :] = jnp.where(lane < K, piece, 0.0)
    mapped = jnp.dot(
        taps[...].astype(jnp.bfloat16), map_ref[...], preferred_element_type=jnp.float32
    )
    for tile in range(3):
        long[tile] = mapped[:, tile * 128 : (tile + 1) * 128]

    row8 = lax.broadcasted_iota(jnp.int32, (8, 128), 0)
    lane8 = lax.broadcasted_iota(jnp.int32, (8, 128), 1)
    low = row8 < 4

    def between(first, last):
        return (lane8 >= first) & (lane8 < last)

    plain = low & between(0, 32)
    by_32 = (low & between(64, 104)) | (~low & between(32, 64))
    by_72 = ~low & between(104, 128)
    end_72 = (low & between(16, 48)) | (~low & between(0, 16))
    end_104 = ~low & between(48, 80)
    row_z = lax.broadcasted_iota(jnp.int32, (128, 128), 0)
    lane_z = lax.broadcasted_iota(jnp.int32, (128, 128), 1)
    inside = lane_z <= row_z
    row_y = lax.broadcasted_iota(jnp.int32, (TOP, 128), 0)
    lane_y = lax.broadcasted_iota(jnp.int32, (TOP, 128), 1)
    after = lane_y >= XO * row_y
    after8 = lane8 >= XO * row8

    def one_term(i, carry):
        slot = i // R
        r = i % R
        row = jnp.broadcast_to(taps[pl.ds(i, 1), :], (8, 128))
        base = pltpu.roll(row, 0, 1, stride=1, stride_axis=0)
        base = jnp.where(low, base, pltpu.roll(base, 124, 1))
        for b in range(0, XB, 2):
            ends = ([], [])
            for c in (b, b + 1):
                turned = [
                    pltpu.roll(base, (XO * c + k) % 128, 1) if (XO * c + k) % 128 else base
                    for k in (0, 32, 72, 104)
                ]
                ends[0].append(
                    jnp.where(plain, turned[0], jnp.where(by_32, turned[1], jnp.where(by_72, turned[2], 0.0)))
                )
                ends[1].append(jnp.where(end_72, turned[2], jnp.where(end_104, turned[3], 0.0)))
            rows = pl.ds(pl.multiple_of(r * (XB * 8) + b * 8, 16), 16)
            a1_ref[slot, rows, 0:128] = jnp.concatenate(ends[0], axis=0).astype(jnp.bfloat16)
            a1_ref[slot, rows, 128:ROWS] = jnp.concatenate(ends[1], axis=0)[:, : ROWS - 128].astype(jnp.bfloat16)
        halves = [
            pltpu.roll(
                jnp.broadcast_to(long[k, pl.ds(NEED * R + i, 1), :], (TOP, 128)),
                0, 1, stride=XO, stride_axis=0,
            )
            for k in (1, 2)
        ]
        zero = jnp.zeros((TOP, 128), jnp.float32)
        tiles = [
            jnp.where(after, halves[0], 0.0),
            jnp.where(after, halves[1], halves[0]),
            jnp.where(after, 0.0, halves[1]),
            zero,
        ]
        for k in range(4):
            width = min(128, EXT * XO - 128 * k)
            a2_ref[i, :, 128 * k : 128 * k + width] = tiles[k][:, :width].astype(jnp.bfloat16)
        ends = [
            jnp.zeros((8, 128), jnp.float32),
            jnp.where(after8, halves[0][:8], 0.0),
            jnp.where(after8, halves[1][:8], halves[0][:8]),
            jnp.where(after8, 0.0, halves[1][:8]),
        ]
        for k in range(4):
            width = min(128, EXT * XO - 128 * k)
            for o in range(0, XO, 2):
                two = jnp.concatenate(
                    [jnp.where(lane8 % XO == c, ends[k], 0.0) for c in (o, o + 1)], axis=0
                )
                a2b_ref[i, 8 * o : 8 * o + 16, 128 * k : 128 * k + width] = two[:, :width].astype(jnp.bfloat16)
        row = jnp.broadcast_to(long[0, pl.ds(2 * NEED * R + i, 1), :], (128, 128))
        turned = pltpu.roll(row, 0, 1, stride=1, stride_axis=0)
        first = jnp.where(inside, turned, 0.0).astype(jnp.bfloat16)
        second = jnp.where(inside, 0.0, turned).astype(jnp.bfloat16)
        start = (r // 2) * (2 * (Z + 2 * HALF))
        own = pl.multiple_of(start + (r % 2) * Z, 128)
        bz_ref[slot, pl.ds(own, 96), :] = first[32:]
        bz_ref[slot, pl.ds(own + 96, 32), :] = second[:32]
        ends = pl.multiple_of(start + 2 * Z + (r % 2) * 2 * HALF, 64)
        bz_ref[slot, pl.ds(ends, 32), :] = first[:32]
        bz_ref[slot, pl.ds(ends + 32, 32), :] = second[32:64]
        return carry

    lax.fori_loop(0, NEED * R, one_term, 0, unroll=4)


def make_bands(listed, table):
    shapes = [
        (NEED, R * XB * 8, ROWS),
        (NEED * R, TOP, EXT * XO),
        (NEED * R, XO * (Y - TOP), EXT * XO),
        (NEED, R * (Z + 2 * HALF), Z),
    ]
    vmem = pl.BlockSpec(memory_space=pltpu.VMEM)
    return pl.pallas_call(
        bands_kernel,
        out_shape=[jax.ShapeDtypeStruct(shape, jnp.bfloat16) for shape in shapes],
        in_specs=[pl.BlockSpec(memory_space=pltpu.SMEM), vmem, vmem],
        out_specs=[vmem] * 4,
        scratch_shapes=[
            pltpu.VMEM((12, 32, 128), jnp.float32),
            pltpu.VMEM((3 * NEED * R, 128), jnp.float32),
            pltpu.VMEM((3, 3 * NEED * R, 128), jnp.float32),
        ],
        compiler_params=pltpu.CompilerParams(vmem_limit_bytes=14 * 1024 * 1024),
    )(listed, table, tap_maps())


def roll_half(value):
    return pltpu.roll(value, 64, 1)


def stage_x(slot, part, a1_ref, put, offset):
    low = lax.broadcasted_iota(jnp.int32, (8, NARROW), 1) < 64
    pairs = part.shape[0] * 2 // 3

    def step(i, carry):
        g = 2 * i
        rhs = jnp.concatenate(
            [part[4 * i], part[4 * i + 1], part[4 * i + 2], part[4 * i + 3], part[pairs + g], part[pairs + g + 1]],
            axis=1,
        )
        made = jnp.dot(a1_ref[slot], rhs, preferred_element_type=jnp.float32)
        base = pl.multiple_of((offset + g) * 16, 32)

        def cell(r, b, k):
            row = (r * XB + b) * 8
            return made[row : row + 8, k * 128 : (k + 1) * 128]

        def place(r, k, column, first, second):
            put(
                r,
                pl.ds(base + k * 16, 16),
                slice(column * 128, (column + 1) * 128),
                jnp.concatenate([first, second], axis=0).astype(jnp.bfloat16),
            )

        for r in range(R):
            for k in range(2):
                for b in range(XB):
                    place(r, k, b, cell(r, b, 2 * k), cell(r, b, 2 * k + 1))
                for c in range(XB // 2):
                    one, two = cell(r, 2 * c, 4 + k), cell(r, 2 * c + 1, 4 + k)
                    place(
                        r, k, XB + c,
                        jnp.where(low, one, roll_half(two)),
                        jnp.where(low, roll_half(one), two),
                    )
        return carry

    lax.fori_loop(0, pairs // 4, step, 0)


def own_kernel(live_ref, own_ref, a1_ref, out_ref):
    def one_slot(slot, carry):
        def put(r, rows, lanes, value):
            out_ref[slot, r, rows, lanes] = value

        stage_x(slot, own_ref, a1_ref, put, 0)
        return carry

    lax.fori_loop(0, live_ref[0], one_slot, 0)


def blur_own(live, own, a1):
    vmem = pl.BlockSpec(memory_space=pltpu.VMEM)
    return pl.pallas_call(
        own_kernel,
        out_shape=jax.ShapeDtypeStruct((NEED, R, Y * XO, LANES), jnp.bfloat16),
        in_specs=[pl.BlockSpec(memory_space=pltpu.SMEM), vmem, vmem],
        out_specs=vmem,
        compiler_params=pltpu.CompilerParams(vmem_limit_bytes=OWN_LIMIT),
        cost_estimate=pl.CostEstimate(flops=8_000_000_000, bytes_accessed=2_000_000, transcendentals=0),
    )(live, own, a1)


def blur_kernel(
    live_ref, left_ref, own_ref, right_ref, a1_ref, a2_ref, a2b_ref, mask_ref, bz_ref,
    weights_ref, slot_ref, out_ref, line_x, line_y, band_y,
):
    out_ref[...] = jnp.zeros_like(out_ref)
    low_y = lax.broadcasted_iota(jnp.int32, (TOP * XO, NARROW), 1) < 64
    low_b = lax.broadcasted_iota(jnp.int32, ((Y - TOP) * XO, NARROW), 1) < 64
    side = HALF * XO

    def one_slot(slot, carry):
        def put(r, rows, lanes, value):
            line_x[r, rows, lanes] = value

        stage_x(slot, left_ref, a1_ref, put, 0)
        stage_x(slot, right_ref, a1_ref, put, 8)

        def pair(q, carry):
            made = []
            for h in range(2):
                r = 2 * q + h
                top = a2_ref[slot * R + r]
                for o in range(XO):
                    band_y[h, o * TOP : (o + 1) * TOP, :] = top * mask_ref[o : o + 1, :]
                band_y[h, TOP * XO :, :] = a2b_ref[slot * R + r]
                lines = jnp.concatenate([line_x[r, :side], own_ref[slot, r], line_x[r, side:]], axis=0)
                made.append(jnp.dot(band_y[h], lines, preferred_element_type=jnp.float32))
            lanes = pl.multiple_of(q * 384, 128)
            tail = pl.ds(lanes + 256, 128)
            for first, count, start, low in ((0, TOP * XO, 0, low_y), (TOP * XO, (Y - TOP) * XO, TOP * X, low_b)):

                def cell(h, column):
                    return made[h][first : first + count, column * 128 : (column + 1) * 128]

                def rows(b):
                    return slice(start + b * count, start + (b + 1) * count)

                for b in range(XB):
                    for h in range(2):
                        line_y[rows(b), pl.ds(lanes + h * 128, 128)] = cell(h, b).astype(jnp.bfloat16)
                for c in range(XB // 2):
                    one, two = cell(0, XB + c), cell(1, XB + c)
                    line_y[rows(2 * c), tail] = jnp.where(low, one, roll_half(two)).astype(jnp.bfloat16)
                    line_y[rows(2 * c + 1), tail] = jnp.where(low, roll_half(one), two).astype(jnp.bfloat16)
            return carry

        lax.fori_loop(0, R // 2, pair, 0)

        done = jnp.dot(line_y[...], bz_ref[slot], preferred_element_type=jnp.float32)
        for low, high, made in ((0, TOP, done[:1280]), (TOP, Y, done[1280:])):
            weight = jnp.zeros((X, high - low, Z), jnp.float32)
            for j in range(2):
                here = slot_ref[j, :, low:high, :] == slot
                weight = weight + jnp.where(here, weights_ref[j, :, low:high, :].astype(jnp.float32), 0.0)
            out_ref[:, low:high, :] += weight * made.reshape(X, high - low, Z)
        return carry

    lax.fori_loop(0, live_ref[0], one_slot, 0)


def blur(live, cells, bands, weights, cell_slot):
    a1, a2, a2b, bz = bands
    left, own, right = cells
    own = blur_own(live, own, a1)
    vmem = pl.BlockSpec(memory_space=pltpu.VMEM)
    mask = same_lane()
    return pl.pallas_call(
        blur_kernel,
        out_shape=jax.ShapeDtypeStruct((X, Y, Z), jnp.float32),
        in_specs=[pl.BlockSpec(memory_space=pltpu.SMEM)] + [vmem] * 10,
        out_specs=vmem,
        scratch_shapes=[
            pltpu.VMEM((R, 2 * HALF * XO, LANES), jnp.bfloat16),
            pltpu.VMEM((1600, 1536), jnp.bfloat16),
            pltpu.VMEM((2, Y * XO, EXT * XO), jnp.bfloat16),
        ],
        compiler_params=pltpu.CompilerParams(vmem_limit_bytes=BLUR_LIMIT),
    )(live, left, own, right, a1, a2, a2b, mask, bz, weights, cell_slot)


def doubled(rows, axis, bit):
    count = lax.axis_size(axis)
    other = lax.ppermute(rows, axis, [(i, i ^ bit) for i in range(count)])
    upper = (lax.axis_index(axis) & bit) != 0
    return jnp.concatenate(
        [jnp.where(upper, other, rows), jnp.where(upper, rows, other)], axis=0
    )


def both_ways(to_next, to_last, axis):
    count = lax.axis_size(axis)
    ends = count - 1
    after = lax.ppermute(to_last, axis, [((i + 1) % count, i) for i in range(ends)])
    before = lax.ppermute(to_next, axis, [(i, (i + 1) % count) for i in range(ends)])
    return before, after


def lane_part():
    return lax.broadcasted_iota(jnp.int32, (1, NARROW), 1) // HALF


def ends_kernel(reflect_ref, factors_ref, shallower_ref, deeper_ref, rows_ref):
    rows_ref[...] = factors_ref[...]
    part = lane_part()
    for g in range(Y // 8):
        rows = [reflect_ref[:, 8 * g + k, :] for k in range(8)]
        for ref, first in ((deeper_ref, Z - HALF), (shallower_ref, 0)):
            packed = []
            for s in range(2):
                value = None
                for k in range(4):
                    shift = (k * HALF - first) % NARROW
                    turned = rows[2 * k + s]
                    turned = pltpu.roll(turned, shift, 1) if shift else turned
                    value = turned if value is None else jnp.where(part == k, turned, value)
                packed.append(value)
            ref[g] = jnp.concatenate(packed, axis=0).astype(jnp.bfloat16)


def depth_ends(reflect, factors):
    vmem = pl.BlockSpec(memory_space=pltpu.VMEM)
    shapes = [(5, 80, NARROW), (5, 80, NARROW), factors.shape]
    return pl.pallas_call(
        ends_kernel,
        out_shape=[jax.ShapeDtypeStruct(shape, jnp.bfloat16) for shape in shapes],
        in_specs=[vmem] * 2,
        out_specs=[vmem] * 3,
        compiler_params=pltpu.CompilerParams(vmem_limit_bytes=SMALL_LIMIT),
    )(reflect, factors)


def cut_kernel(reflect_ref, after_ref, own_ref, next_ref, last_ref):
    for pair in range(Y // 2):
        two = [reflect_ref[:, 2 * pair + k, :] for k in range(2)]
        own_ref[pair] = jnp.concatenate(two, axis=0).astype(jnp.bfloat16)
        next_ref[pair] = jnp.concatenate([v[X - HALF :] for v in two], axis=0).astype(jnp.bfloat16)
        last_ref[pair] = jnp.concatenate([v[:HALF] for v in two], axis=0).astype(jnp.bfloat16)


def cut(reflect, after):
    shapes = [(20, 80, Z), (20, 64, Z), (20, 64, Z)]
    vmem = pl.BlockSpec(memory_space=pltpu.VMEM)
    return pl.pallas_call(
        cut_kernel,
        out_shape=[jax.ShapeDtypeStruct(shape, jnp.bfloat16) for shape in shapes],
        in_specs=[vmem, pl.BlockSpec(memory_space=pl.ANY)],
        out_specs=[vmem] * 3,
        compiler_params=pltpu.CompilerParams(vmem_limit_bytes=SMALL_LIMIT),
        cost_estimate=pl.CostEstimate(flops=8_000_000_000, bytes_accessed=2_000_000, transcendentals=0),
    )(reflect, after)


def tail_kernel(left_ref, right_ref, main_next, main_last, own_ref, next_ref, last_ref):
    part = lane_part()
    next_ref[:20] = main_next[...]
    last_ref[:20] = main_last[...]
    for g in range(5):
        left = left_ref[g].astype(jnp.float32)
        right = right_ref[g].astype(jnp.float32)
        for a in range(2):
            value = left if a == 0 else pltpu.roll(left, 64, 1)
            for k, (source, at) in enumerate(((right, 2 * a), (left, 2 * a + 1), (right, 2 * a + 1)), 1):
                shift = ((k - at) * HALF) % NARROW
                turned = pltpu.roll(source, shift, 1) if shift else source
                value = jnp.where(part == k, turned, value)
            own_ref[2 * g + a] = value.astype(jnp.bfloat16)
            next_ref[20 + 2 * g + a] = jnp.concatenate(
                [value[X - HALF : X], value[2 * X - HALF :]], axis=0
            ).astype(jnp.bfloat16)
            last_ref[20 + 2 * g + a] = jnp.concatenate(
                [value[:HALF], value[X : X + HALF]], axis=0
            ).astype(jnp.bfloat16)


def unpack_tail(left, right, main_next, main_last):
    shapes = [(10, 80, NARROW), (30, 64, NARROW), (30, 64, NARROW)]
    vmem = pl.BlockSpec(memory_space=pltpu.VMEM)
    return pl.pallas_call(
        tail_kernel,
        out_shape=[jax.ShapeDtypeStruct(shape, jnp.bfloat16) for shape in shapes],
        in_specs=[vmem] * 4,
        out_specs=[vmem] * 3,
        compiler_params=pltpu.CompilerParams(vmem_limit_bytes=SMALL_LIMIT),
    )(left, right, main_next, main_last)


def join_kernel(before_ref, own_ref, tail_ref, after_ref, rows_ref, all_ref, next_ref, last_ref):
    for ref, to, at, count in (
        (all_ref, 0, 0, 30),
        (next_ref, 0, 4, 16),
        (next_ref, 16, 22, 8),
        (last_ref, 0, 0, 16),
        (last_ref, 16, 20, 8),
    ):
        ref[to : to + count, 0:64, :] = before_ref[at : at + count]
        ref[to : to + count, 144:208, :] = after_ref[at : at + count]
        mains = min(max(20 - at, 0), count)
        if mains:
            ref[to : to + mains, 64:144, :] = own_ref[at : at + mains]
        if count > mains:
            first = max(at - 20, 0)
            ref[to + mains : to + count, 64:144, :] = tail_ref[first : first + count - mains]


def join(before, own, tail, after, rows):
    vmem = pl.BlockSpec(memory_space=pltpu.VMEM)
    return pl.pallas_call(
        join_kernel,
        out_shape=[jax.ShapeDtypeStruct((n, ROWS, NARROW), jnp.bfloat16) for n in (30, 24, 24)],
        in_specs=[vmem] * 4 + [pl.BlockSpec(memory_space=pl.ANY)],
        out_specs=[vmem] * 3,
        compiler_params=pltpu.CompilerParams(vmem_limit_bytes=12 * 1024 * 1024),
    )(before, own, tail, after, rows)


def exchange(reflect, factors):
    shallower, deeper, rows = depth_ends(reflect, factors)
    above, below = both_ways(deeper, shallower, "gz")
    own, to_next, to_last = cut(reflect, deeper)
    rows = doubled(doubled(rows, "xl", 1), "xl", 2)
    tail, to_next, to_last = unpack_tail(above, below, to_next, to_last)
    before, after = both_ways(to_next, to_last, "il")
    block, to_next, to_last = join(before, own, tail, after, rows)
    rows = doubled(rows, "xl", 4)
    left, right = both_ways(to_next, to_last, "xl")
    return (left, block, right), rows


def per_device(reflect, weights, cell_slot, factors, reader_list):
    listed = reader_list.reshape(NEED)
    live_count = jnp.sum((listed >= 0).astype(jnp.int32))
    cells, rows = exchange(reflect, factors)
    bands = make_bands(listed, rows)
    return blur(live_count.reshape(1), cells, bands, weights, cell_slot)


def solution(mesh):
    in_specs = (
        P("il", "xl", "gz"),
        P(None, "il", "xl", "gz"),
        P(None, "il", "xl", "gz"),
        P(("il", "xl", "gz"), None),
        P("il", "xl", "gz", None),
    )
    out_specs = P("il", "xl", "gz")
    return jax.shard_map(
        per_device, mesh=mesh, in_specs=in_specs, out_specs=out_specs, check_vma=False
    )
```

```python
import jax
import jax.numpy as jnp
import numpy as np
from jax import lax
from jax.experimental import pallas as pl
from jax.experimental.pallas import tpu as pltpu
from jax.sharding import PartitionSpec as P

K = 64
R = 8
CP_DEV = 4
NEED = 3
HALF = 32
X, Y, Z = 40, 40, 128
XO = 4
XB = X // XO
LANES = XB * 192
SMALL_LIMIT = 10 * 1024 * 1024
OWN_LIMIT = 24 * 1024 * 1024
BLUR_LIMIT = 22 * 1024 * 1024
EXT = 104
ROWS = 2 * EXT
NARROW = 128
TOP = 32


def same_lane():
    return jnp.asarray(np.arange(EXT * XO)[None, :] % XO == np.arange(XO)[:, None], jnp.bfloat16)


def tap_maps():
    reverse = np.zeros((128, 128), np.float32)
    repeat = np.zeros((128, 256), np.float32)
    for t in range(K):
        reverse[t, -t % 128] = 1
        repeat[t, XO * t : XO * (t + 1)] = 1
    return jnp.asarray(np.concatenate([reverse, repeat], axis=1), jnp.bfloat16)


def bands_kernel(list_ref, table_ref, map_ref, a1_ref, a2_ref, a2b_ref, bz_ref, table, taps, long):
    for tile in range(12):
        table[tile] = table_ref[:, tile * 128 : (tile + 1) * 128].astype(jnp.float32)
    lane = lax.broadcasted_iota(jnp.int32, (1, 128), 1)
    for slot in range(NEED):
        listed = jnp.maximum(list_ref[slot], 0)
        key = (listed // (CP_DEV * 8)) % 8 * CP_DEV + listed % CP_DEV
        for r in range(R):
            for axis in range(3):
                tile, half = divmod(3 * r + axis, 2)
                piece = table[tile, pl.ds(key, 1), :]
                if half:
                    piece = pltpu.roll(piece, 64, 1)
                at = axis * NEED * R + slot * R + r
                taps[at : at + 1, :] = jnp.where(lane < K, piece, 0.0)
    mapped = jnp.dot(
        taps[...].astype(jnp.bfloat16), map_ref[...], preferred_element_type=jnp.float32
    )
    for tile in range(3):
        long[tile] = mapped[:, tile * 128 : (tile + 1) * 128]

    row8 = lax.broadcasted_iota(jnp.int32, (8, 128), 0)
    lane8 = lax.broadcasted_iota(jnp.int32, (8, 128), 1)
    low = row8 < 4

    def between(first, last):
        return (lane8 >= first) & (lane8 < last)

    parts = (
        (96, low & between(0, 40), None),
        (8, ~low & between(40, 80), None),
        (80, low & between(80, 112), None),
        (112, ~low & between(112, 128), ~low & between(0, 16)),
        (72, None, low & between(16, 48)),
        (104, None, ~low & between(48, 80)),
    )
    row_z = lax.broadcasted_iota(jnp.int32, (128, 128), 0)
    lane_z = lax.broadcasted_iota(jnp.int32, (128, 128), 1)
    inside = lane_z <= row_z
    row_y = lax.broadcasted_iota(jnp.int32, (TOP, 128), 0)
    lane_y = lax.broadcasted_iota(jnp.int32, (TOP, 128), 1)
    after = lane_y >= XO * row_y
    after8 = lane8 >= XO * row8

    def one_term(i, carry):
        slot = i // R
        r = i % R
        row = jnp.broadcast_to(taps[pl.ds(i, 1), :], (8, 128))
        base = pltpu.roll(row, 0, 1, stride=1, stride_axis=0)
        base = jnp.where(low, base, pltpu.roll(base, 124, 1))
        for b in range(0, XB, 2):
            ends = ([], [])
            for c in (b, b + 1):
                first = second = jnp.zeros((8, 128), jnp.float32)
                for shift, here, there in parts:
                    turned = pltpu.roll(base, (XO * c + shift) % 128, 1) if (XO * c + shift) % 128 else base
                    first = first if here is None else jnp.where(here, turned, first)
                    second = second if there is None else jnp.where(there, turned, second)
                ends[0].append(first)
                ends[1].append(second)
            rows = pl.ds(pl.multiple_of(r * (XB * 8) + b * 8, 16), 16)
            a1_ref[slot, rows, 0:128] = jnp.concatenate(ends[0], axis=0).astype(jnp.bfloat16)
            a1_ref[slot, rows, 128:ROWS] = jnp.concatenate(ends[1], axis=0)[:, : ROWS - 128].astype(jnp.bfloat16)
        halves = [
            pltpu.roll(
                jnp.broadcast_to(long[k, pl.ds(NEED * R + i, 1), :], (TOP, 128)),
                0, 1, stride=XO, stride_axis=0,
            )
            for k in (1, 2)
        ]
        zero = jnp.zeros((TOP, 128), jnp.float32)
        tiles = [
            jnp.where(after, halves[0], 0.0),
            jnp.where(after, halves[1], halves[0]),
            jnp.where(after, 0.0, halves[1]),
            zero,
        ]
        for k in range(4):
            width = min(128, EXT * XO - 128 * k)
            a2_ref[i, :, 128 * k : 128 * k + width] = tiles[k][:, :width].astype(jnp.bfloat16)
        ends = [
            jnp.zeros((8, 128), jnp.float32),
            jnp.where(after8, halves[0][:8], 0.0),
            jnp.where(after8, halves[1][:8], halves[0][:8]),
            jnp.where(after8, 0.0, halves[1][:8]),
        ]
        for k in range(4):
            width = min(128, EXT * XO - 128 * k)
            for o in range(0, XO, 2):
                two = jnp.concatenate(
                    [jnp.where(lane8 % XO == c, ends[k], 0.0) for c in (o, o + 1)], axis=0
                )
                a2b_ref[i, 8 * o : 8 * o + 16, 128 * k : 128 * k + width] = two[:, :width].astype(jnp.bfloat16)
        row = jnp.broadcast_to(long[0, pl.ds(2 * NEED * R + i, 1), :], (128, 128))
        turned = pltpu.roll(row, 0, 1, stride=1, stride_axis=0)
        first = jnp.where(inside, turned, 0.0).astype(jnp.bfloat16)
        second = jnp.where(inside, 0.0, turned).astype(jnp.bfloat16)
        start = (r // 2) * (2 * (Z + 2 * HALF))
        own = pl.multiple_of(start + (r % 2) * Z, 128)
        bz_ref[slot, pl.ds(own, 96), :] = first[32:]
        bz_ref[slot, pl.ds(own + 96, 32), :] = second[:32]
        ends = pl.multiple_of(start + 2 * Z + (r % 2) * 2 * HALF, 64)
        bz_ref[slot, pl.ds(ends, 32), :] = first[:32]
        bz_ref[slot, pl.ds(ends + 32, 32), :] = second[32:64]
        return carry

    lax.fori_loop(0, NEED * R, one_term, 0, unroll=4)


def make_bands(listed, table):
    shapes = [
        (NEED, R * XB * 8, ROWS),
        (NEED * R, TOP, EXT * XO),
        (NEED * R, XO * (Y - TOP), EXT * XO),
        (NEED, R * (Z + 2 * HALF), Z),
    ]
    vmem = pl.BlockSpec(memory_space=pltpu.VMEM)
    return pl.pallas_call(
        bands_kernel,
        out_shape=[jax.ShapeDtypeStruct(shape, jnp.bfloat16) for shape in shapes],
        in_specs=[pl.BlockSpec(memory_space=pltpu.SMEM), vmem, vmem],
        out_specs=[vmem] * 4,
        scratch_shapes=[
            pltpu.VMEM((12, 32, 128), jnp.float32),
            pltpu.VMEM((3 * NEED * R, 128), jnp.float32),
            pltpu.VMEM((3, 3 * NEED * R, 128), jnp.float32),
        ],
        compiler_params=pltpu.CompilerParams(vmem_limit_bytes=14 * 1024 * 1024),
    )(listed, table, tap_maps())


def roll_half(value):
    return pltpu.roll(value, 64, 1)


def stage_x(slot, pairs, fetch, a1_ref, put, offset):
    low = lax.broadcasted_iota(jnp.int32, (8, NARROW), 1) < 64

    def step(i, carry):
        g = 2 * i
        rhs = jnp.concatenate(
            [fetch(4 * i + k) for k in range(4)] + [fetch(pairs + g + k) for k in range(2)],
            axis=1,
        )
        made = jnp.dot(a1_ref[slot], rhs, preferred_element_type=jnp.float32)
        base = pl.multiple_of((offset + g) * 16, 32)

        def cell(r, b, k):
            row = (r * XB + b) * 8
            return made[row : row + 8, k * 128 : (k + 1) * 128]

        def place(r, k, column, first, second):
            put(
                r,
                pl.ds(base + k * 16, 16),
                slice(column * 128, (column + 1) * 128),
                jnp.concatenate([first, second], axis=0).astype(jnp.bfloat16),
            )

        for r in range(R):
            for k in range(2):
                for b in range(XB):
                    place(r, k, b, cell(r, b, 2 * k), cell(r, b, 2 * k + 1))
                for c in range(XB // 2):
                    one, two = cell(r, 2 * c, 4 + k), cell(r, 2 * c + 1, 4 + k)
                    place(
                        r, k, XB + c,
                        jnp.where(low, one, roll_half(two)),
                        jnp.where(low, roll_half(one), two),
                    )
        return carry

    lax.fori_loop(0, pairs // 4, step, 0)


def own_kernel(live_ref, cells_ref, tail_ref, before_ref, after_ref, a1_ref, out_ref, own_ref):
    own_ref[:20] = cells_ref[...]
    own_ref[20:] = tail_ref[...]

    def fetch(i):
        return jnp.concatenate([own_ref[i], before_ref[i], after_ref[i]], axis=0)

    def one_slot(slot, carry):
        def put(r, rows, lanes, value):
            out_ref[slot, r, rows, lanes] = value

        stage_x(slot, 20, fetch, a1_ref, put, 0)
        return carry

    lax.fori_loop(0, live_ref[0], one_slot, 0)


def blur_own(live, cells, a1):
    vmem = pl.BlockSpec(memory_space=pltpu.VMEM)
    return pl.pallas_call(
        own_kernel,
        out_shape=jax.ShapeDtypeStruct((NEED, R, Y * XO, LANES), jnp.bfloat16),
        in_specs=[pl.BlockSpec(memory_space=pltpu.SMEM)] + [vmem] * 5,
        out_specs=vmem,
        scratch_shapes=[pltpu.VMEM((30, 80, NARROW), jnp.bfloat16)],
        compiler_params=pltpu.CompilerParams(vmem_limit_bytes=OWN_LIMIT),
        cost_estimate=pl.CostEstimate(flops=8_000_000_000, bytes_accessed=2_000_000, transcendentals=0),
    )(live, *cells, a1)


def blur_kernel(
    live_ref, left_ref, left_ends, right_ref, right_ends, own_ref, a1_ref, a2_ref, a2b_ref, mask_ref, bz_ref,
    weights_ref, slot_ref, out_ref, line_x, line_y, band_y,
):
    out_ref[...] = jnp.zeros_like(out_ref)
    low_y = lax.broadcasted_iota(jnp.int32, (TOP * XO, NARROW), 1) < 64
    low_b = lax.broadcasted_iota(jnp.int32, ((Y - TOP) * XO, NARROW), 1) < 64
    side = HALF * XO

    def one_slot(slot, carry):
        def put(r, rows, lanes, value):
            line_x[r, rows, lanes] = value

        for cells, ends, offset in ((left_ref, left_ends, 0), (right_ref, right_ends, 8)):

            def fetch(i):
                return jnp.concatenate([cells[i], ends[i]], axis=0)

            stage_x(slot, 16, fetch, a1_ref, put, offset)

        def pair(q, carry):
            made = []
            for h in range(2):
                r = 2 * q + h
                top = a2_ref[slot * R + r]
                for o in range(XO):
                    band_y[h, o * TOP : (o + 1) * TOP, :] = top * mask_ref[o : o + 1, :]
                band_y[h, TOP * XO :, :] = a2b_ref[slot * R + r]
                lines = jnp.concatenate([line_x[r, :side], own_ref[slot, r], line_x[r, side:]], axis=0)
                made.append(jnp.dot(band_y[h], lines, preferred_element_type=jnp.float32))
            lanes = pl.multiple_of(q * 384, 128)
            tail = pl.ds(lanes + 256, 128)
            for first, count, start, low in ((0, TOP * XO, 0, low_y), (TOP * XO, (Y - TOP) * XO, TOP * X, low_b)):

                def cell(h, column):
                    return made[h][first : first + count, column * 128 : (column + 1) * 128]

                def rows(b):
                    return slice(start + b * count, start + (b + 1) * count)

                for b in range(XB):
                    for h in range(2):
                        line_y[rows(b), pl.ds(lanes + h * 128, 128)] = cell(h, b).astype(jnp.bfloat16)
                for c in range(XB // 2):
                    one, two = cell(0, XB + c), cell(1, XB + c)
                    line_y[rows(2 * c), tail] = jnp.where(low, one, roll_half(two)).astype(jnp.bfloat16)
                    line_y[rows(2 * c + 1), tail] = jnp.where(low, roll_half(one), two).astype(jnp.bfloat16)
            return carry

        lax.fori_loop(0, R // 2, pair, 0)

        done = jnp.dot(line_y[...], bz_ref[slot], preferred_element_type=jnp.float32)
        for low, high, made in ((0, TOP, done[:1280]), (TOP, Y, done[1280:])):
            weight = jnp.zeros((X, high - low, Z), jnp.float32)
            for j in range(2):
                here = slot_ref[j, :, low:high, :] == slot
                weight = weight + jnp.where(here, weights_ref[j, :, low:high, :].astype(jnp.float32), 0.0)
            out_ref[:, low:high, :] += weight * made.reshape(X, high - low, Z)
        return carry

    lax.fori_loop(0, live_ref[0], one_slot, 0)


def blur(live, cells, bands, weights, cell_slot):
    a1, a2, a2b, bz = bands
    inside, sides = cells
    own = blur_own(live, inside, a1)
    vmem = pl.BlockSpec(memory_space=pltpu.VMEM)
    mask = same_lane()
    return pl.pallas_call(
        blur_kernel,
        out_shape=jax.ShapeDtypeStruct((X, Y, Z), jnp.float32),
        in_specs=[pl.BlockSpec(memory_space=pltpu.SMEM)] + [vmem] * 12,
        out_specs=vmem,
        scratch_shapes=[
            pltpu.VMEM((R, 2 * HALF * XO, LANES), jnp.bfloat16),
            pltpu.VMEM((1600, 1536), jnp.bfloat16),
            pltpu.VMEM((2, Y * XO, EXT * XO), jnp.bfloat16),
        ],
        compiler_params=pltpu.CompilerParams(vmem_limit_bytes=BLUR_LIMIT),
    )(live, *sides, own, a1, a2, a2b, mask, bz, weights, cell_slot)


def doubled(rows, axis, bit):
    count = lax.axis_size(axis)
    other = lax.ppermute(rows, axis, [(i, i ^ bit) for i in range(count)])
    upper = (lax.axis_index(axis) & bit) != 0
    return jnp.concatenate(
        [jnp.where(upper, other, rows), jnp.where(upper, rows, other)], axis=0
    )


def both_ways(to_next, to_last, axis):
    count = lax.axis_size(axis)
    ends = count - 1
    after = lax.ppermute(to_last, axis, [((i + 1) % count, i) for i in range(ends)])
    before = lax.ppermute(to_next, axis, [(i, (i + 1) % count) for i in range(ends)])
    return before, after


def lane_part():
    return lax.broadcasted_iota(jnp.int32, (1, NARROW), 1) // HALF


def ends_kernel(reflect_ref, shallower_ref, deeper_ref):
    part = lane_part()
    for g in range(Y // 8):
        rows = [reflect_ref[:, 8 * g + k, :] for k in range(8)]
        for ref, first in ((deeper_ref, Z - HALF), (shallower_ref, 0)):
            packed = []
            for s in range(2):
                value = None
                for k in range(4):
                    shift = (k * HALF - first) % NARROW
                    turned = rows[2 * k + s]
                    turned = pltpu.roll(turned, shift, 1) if shift else turned
                    value = turned if value is None else jnp.where(part == k, turned, value)
                packed.append(value)
            ref[g] = jnp.concatenate(packed, axis=0).astype(jnp.bfloat16)


def depth_ends(reflect):
    vmem = pl.BlockSpec(memory_space=pltpu.VMEM)
    shapes = [(5, 80, NARROW), (5, 80, NARROW)]
    return pl.pallas_call(
        ends_kernel,
        out_shape=[jax.ShapeDtypeStruct(shape, jnp.bfloat16) for shape in shapes],
        in_specs=[vmem],
        out_specs=[vmem] * 2,
        compiler_params=pltpu.CompilerParams(vmem_limit_bytes=SMALL_LIMIT),
    )(reflect)


def cut_kernel(reflect_ref, after_ref, own_ref, next_ref, last_ref):
    for pair in range(Y // 2):
        two = [reflect_ref[:, 2 * pair + k, :] for k in range(2)]
        own_ref[pair] = jnp.concatenate(two, axis=0).astype(jnp.bfloat16)
        next_ref[pair] = jnp.concatenate([v[X - HALF :] for v in two], axis=0).astype(jnp.bfloat16)
        last_ref[pair] = jnp.concatenate([v[:HALF] for v in two], axis=0).astype(jnp.bfloat16)


def cut(reflect, after):
    shapes = [(20, 80, Z), (20, 64, Z), (20, 64, Z)]
    vmem = pl.BlockSpec(memory_space=pltpu.VMEM)
    return pl.pallas_call(
        cut_kernel,
        out_shape=[jax.ShapeDtypeStruct(shape, jnp.bfloat16) for shape in shapes],
        in_specs=[vmem, pl.BlockSpec(memory_space=pl.ANY)],
        out_specs=[vmem] * 3,
        compiler_params=pltpu.CompilerParams(vmem_limit_bytes=SMALL_LIMIT),
        cost_estimate=pl.CostEstimate(flops=8_000_000_000, bytes_accessed=2_000_000, transcendentals=0),
    )(reflect, after)


def tail_kernel(
    left_ref, right_ref, cells_ref, main_next, main_last, own_ref, next_ref, last_ref, across_next, across_last
):
    part = lane_part()
    across_next[:16] = cells_ref[4:]
    across_last[:16] = cells_ref[:16]
    next_ref[:20] = main_next[...]
    last_ref[:20] = main_last[...]
    for g in range(5):
        left = left_ref[g].astype(jnp.float32)
        right = right_ref[g].astype(jnp.float32)
        for a in range(2):
            value = left if a == 0 else pltpu.roll(left, 64, 1)
            for k, (source, at) in enumerate(((right, 2 * a), (left, 2 * a + 1), (right, 2 * a + 1)), 1):
                shift = ((k - at) * HALF) % NARROW
                turned = pltpu.roll(source, shift, 1) if shift else source
                value = jnp.where(part == k, turned, value)
            tail = value.astype(jnp.bfloat16)
            own_ref[2 * g + a] = tail
            if g > 0:
                across_next[16 + 2 * g + a - 2] = tail
            if g < 4:
                across_last[16 + 2 * g + a] = tail
            next_ref[20 + 2 * g + a] = jnp.concatenate(
                [value[X - HALF : X], value[2 * X - HALF :]], axis=0
            ).astype(jnp.bfloat16)
            last_ref[20 + 2 * g + a] = jnp.concatenate(
                [value[:HALF], value[X : X + HALF]], axis=0
            ).astype(jnp.bfloat16)


def unpack_tail(left, right, own, main_next, main_last):
    shapes = [(10, 80), (30, 64), (30, 64), (24, 80), (24, 80)]
    vmem = pl.BlockSpec(memory_space=pltpu.VMEM)
    return pl.pallas_call(
        tail_kernel,
        out_shape=[jax.ShapeDtypeStruct(shape + (NARROW,), jnp.bfloat16) for shape in shapes],
        in_specs=[vmem] * 5,
        out_specs=[vmem] * 5,
        compiler_params=pltpu.CompilerParams(vmem_limit_bytes=SMALL_LIMIT),
    )(left, right, own, main_next, main_last)


def join_kernel(before_ref, after_ref, rows_ref, left_ref, right_ref, next_ref, last_ref):
    for ref, to, at, count in (
        (next_ref, 0, 4, 16),
        (next_ref, 16, 22, 8),
        (last_ref, 0, 0, 16),
        (last_ref, 16, 20, 8),
    ):
        ref[to : to + count, 0:64, :] = before_ref[at : at + count]
        ref[to : to + count, 64:128, :] = after_ref[at : at + count]


def join(before, after, rows, left, right):
    vmem = pl.BlockSpec(memory_space=pltpu.VMEM)
    return pl.pallas_call(
        join_kernel,
        out_shape=[jax.ShapeDtypeStruct((24, 128, NARROW), jnp.bfloat16)] * 2,
        in_specs=[vmem] * 2 + [pl.BlockSpec(memory_space=pl.ANY)] * 3,
        out_specs=[vmem] * 2,
        compiler_params=pltpu.CompilerParams(vmem_limit_bytes=SMALL_LIMIT),
    )(before, after, rows, left, right)


def exchange(reflect, factors):
    shallower, deeper = depth_ends(reflect)
    above, below = both_ways(deeper, shallower, "gz")
    rows = doubled(factors, "xl", 1)
    own, to_next, to_last = cut(reflect, shallower)
    rows = doubled(rows, "xl", 2)
    tail, to_next, to_last, across_next, across_last = unpack_tail(above, below, own, to_next, to_last)
    before, after = both_ways(to_next, to_last, "il")
    left, right = both_ways(across_next, across_last, "xl")
    to_next, to_last = join(before, after, rows, left, right)
    left_ends, right_ends = both_ways(to_next, to_last, "xl")
    rows = doubled(rows, "xl", 4)
    return ((own, tail, before, after), (left, left_ends, right, right_ends)), rows


def per_device(reflect, weights, cell_slot, factors, reader_list):
    listed = reader_list.reshape(NEED)
    live_count = jnp.sum((listed >= 0).astype(jnp.int32))
    cells, rows = exchange(reflect, factors)
    bands = make_bands(listed, rows)
    return blur(live_count.reshape(1), cells, bands, weights, cell_slot)


def solution(mesh):
    in_specs = (
        P("il", "xl", "gz"),
        P(None, "il", "xl", "gz"),
        P(None, "il", "xl", "gz"),
        P(("il", "xl", "gz"), None),
        P("il", "xl", "gz", None),
    )
    out_specs = P("il", "xl", "gz")
    return jax.shard_map(
        per_device, mesh=mesh, in_specs=in_specs, out_specs=out_specs, check_vma=False
    )
```

```python
import jax
import jax.numpy as jnp
import numpy as np
from jax import lax
from jax.experimental import pallas as pl
from jax.experimental.pallas import tpu as pltpu
from jax.sharding import PartitionSpec as P

K = 64
R = 8
CP_DEV = 4
NEED = 3
HALF = 32
X, Y, Z = 40, 40, 128
XO = 4
XB = X // XO
LANES = XB * 192
SMALL_LIMIT = 10 * 1024 * 1024
OWN_LIMIT = 24 * 1024 * 1024
BLUR_LIMIT = 22 * 1024 * 1024
EXT = 104
ROWS = 2 * EXT
NARROW = 128
TOP = 32


def same_lane():
    return jnp.asarray(np.arange(EXT * XO)[None, :] % XO == np.arange(XO)[:, None], jnp.bfloat16)


def tap_maps():
    reverse = np.zeros((128, 128), np.float32)
    repeat = np.zeros((128, 256), np.float32)
    for t in range(K):
        reverse[t, -t % 128] = 1
        repeat[t, XO * t : XO * (t + 1)] = 1
    return jnp.asarray(np.concatenate([reverse, repeat], axis=1), jnp.bfloat16)


def bands_kernel(list_ref, table_ref, map_ref, a1_ref, a2_ref, a2b_ref, bz_ref, table, taps, long):
    for tile in range(12):
        table[tile] = table_ref[:, tile * 128 : (tile + 1) * 128].astype(jnp.float32)
    lane = lax.broadcasted_iota(jnp.int32, (1, 128), 1)
    for slot in range(NEED):
        listed = jnp.maximum(list_ref[slot], 0)
        key = (listed // (CP_DEV * 8)) % 8 * CP_DEV + listed % CP_DEV
        for r in range(R):
            for axis in range(3):
                tile, half = divmod(3 * r + axis, 2)
                piece = table[tile, pl.ds(key, 1), :]
                if half:
                    piece = pltpu.roll(piece, 64, 1)
                at = axis * NEED * R + slot * R + r
                taps[at : at + 1, :] = jnp.where(lane < K, piece, 0.0)
    mapped = jnp.dot(
        taps[...].astype(jnp.bfloat16), map_ref[...], preferred_element_type=jnp.float32
    )
    for tile in range(3):
        long[tile] = mapped[:, tile * 128 : (tile + 1) * 128]

    row8 = lax.broadcasted_iota(jnp.int32, (8, 128), 0)
    lane8 = lax.broadcasted_iota(jnp.int32, (8, 128), 1)
    low = row8 < 4

    def between(first, last):
        return (lane8 >= first) & (lane8 < last)

    parts = (
        (96, low & between(0, 40), None),
        (8, ~low & between(40, 80), None),
        (80, low & between(80, 112), None),
        (112, ~low & between(112, 128), ~low & between(0, 16)),
        (72, None, low & between(16, 48)),
        (104, None, ~low & between(48, 80)),
    )
    row_z = lax.broadcasted_iota(jnp.int32, (128, 128), 0)
    lane_z = lax.broadcasted_iota(jnp.int32, (128, 128), 1)
    inside = lane_z <= row_z
    row_y = lax.broadcasted_iota(jnp.int32, (TOP, 128), 0)
    lane_y = lax.broadcasted_iota(jnp.int32, (TOP, 128), 1)
    after = lane_y >= XO * row_y
    after8 = lane8 >= XO * row8

    def one_term(i, carry):
        slot = i // R
        r = i % R
        row = jnp.broadcast_to(taps[pl.ds(i, 1), :], (8, 128))
        base = pltpu.roll(row, 0, 1, stride=1, stride_axis=0)
        base = jnp.where(low, base, pltpu.roll(base, 124, 1))
        for b in range(0, XB, 2):
            ends = ([], [])
            for c in (b, b + 1):
                first = second = jnp.zeros((8, 128), jnp.float32)
                for shift, here, there in parts:
                    turned = pltpu.roll(base, (XO * c + shift) % 128, 1) if (XO * c + shift) % 128 else base
                    first = first if here is None else jnp.where(here, turned, first)
                    second = second if there is None else jnp.where(there, turned, second)
                ends[0].append(first)
                ends[1].append(second)
            rows = pl.ds(pl.multiple_of(r * (XB * 8) + b * 8, 16), 16)
            a1_ref[slot, rows, 0:128] = jnp.concatenate(ends[0], axis=0).astype(jnp.bfloat16)
            a1_ref[slot, rows, 128:ROWS] = jnp.concatenate(ends[1], axis=0)[:, : ROWS - 128].astype(jnp.bfloat16)
        halves = [
            pltpu.roll(
                jnp.broadcast_to(long[k, pl.ds(NEED * R + i, 1), :], (TOP, 128)),
                0, 1, stride=XO, stride_axis=0,
            )
            for k in (1, 2)
        ]
        zero = jnp.zeros((TOP, 128), jnp.float32)
        tiles = [
            jnp.where(after, halves[0], 0.0),
            jnp.where(after, halves[1], halves[0]),
            jnp.where(after, 0.0, halves[1]),
            zero,
        ]
        for k in range(4):
            width = min(128, EXT * XO - 128 * k)
            a2_ref[i, :, 128 * k : 128 * k + width] = tiles[k][:, :width].astype(jnp.bfloat16)
        ends = [
            jnp.zeros((8, 128), jnp.float32),
            jnp.where(after8, halves[0][:8], 0.0),
            jnp.where(after8, halves[1][:8], halves[0][:8]),
            jnp.where(after8, 0.0, halves[1][:8]),
        ]
        for k in range(4):
            width = min(128, EXT * XO - 128 * k)
            for o in range(0, XO, 2):
                two = jnp.concatenate(
                    [jnp.where(lane8 % XO == c, ends[k], 0.0) for c in (o, o + 1)], axis=0
                )
                a2b_ref[i, 8 * o : 8 * o + 16, 128 * k : 128 * k + width] = two[:, :width].astype(jnp.bfloat16)
        row = jnp.broadcast_to(long[0, pl.ds(2 * NEED * R + i, 1), :], (128, 128))
        turned = pltpu.roll(row, 0, 1, stride=1, stride_axis=0)
        first = jnp.where(inside, turned, 0.0).astype(jnp.bfloat16)
        second = jnp.where(inside, 0.0, turned).astype(jnp.bfloat16)
        start = (r // 2) * (2 * (Z + 2 * HALF))
        own = pl.multiple_of(start + (r % 2) * Z, 128)
        bz_ref[slot, pl.ds(own, 96), :] = first[32:]
        bz_ref[slot, pl.ds(own + 96, 32), :] = second[:32]
        ends = pl.multiple_of(start + 2 * Z + (r % 2) * 2 * HALF, 64)
        bz_ref[slot, pl.ds(ends, 32), :] = first[:32]
        bz_ref[slot, pl.ds(ends + 32, 32), :] = second[32:64]
        return carry

    lax.fori_loop(0, NEED * R, one_term, 0, unroll=4)


def make_bands(listed, table):
    shapes = [
        (NEED, R * XB * 8, ROWS),
        (NEED * R, TOP, EXT * XO),
        (NEED * R, XO * (Y - TOP), EXT * XO),
        (NEED, R * (Z + 2 * HALF), Z),
    ]
    vmem = pl.BlockSpec(memory_space=pltpu.VMEM)
    return pl.pallas_call(
        bands_kernel,
        out_shape=[jax.ShapeDtypeStruct(shape, jnp.bfloat16) for shape in shapes],
        in_specs=[pl.BlockSpec(memory_space=pltpu.SMEM), vmem, vmem],
        out_specs=[vmem] * 4,
        scratch_shapes=[
            pltpu.VMEM((12, 32, 128), jnp.float32),
            pltpu.VMEM((3 * NEED * R, 128), jnp.float32),
            pltpu.VMEM((3, 3 * NEED * R, 128), jnp.float32),
        ],
        compiler_params=pltpu.CompilerParams(vmem_limit_bytes=14 * 1024 * 1024),
        cost_estimate=pl.CostEstimate(flops=8000000000, bytes_accessed=2_000_000, transcendentals=0),
    )(listed, table, tap_maps())


def roll_half(value):
    return pltpu.roll(value, 64, 1)


def stage_x(slot, pairs, fetch, a1_ref, put, offset):
    low = lax.broadcasted_iota(jnp.int32, (8, NARROW), 1) < 64

    def step(i, carry):
        g = 2 * i
        rhs = jnp.concatenate(
            [fetch(4 * i + k) for k in range(4)] + [fetch(pairs + g + k) for k in range(2)],
            axis=1,
        )
        made = jnp.dot(a1_ref[slot], rhs, preferred_element_type=jnp.float32)
        base = pl.multiple_of((offset + g) * 16, 32)

        def cell(r, b, k):
            row = (r * XB + b) * 8
            return made[row : row + 8, k * 128 : (k + 1) * 128]

        def place(r, k, column, first, second):
            put(
                r,
                pl.ds(base + k * 16, 16),
                slice(column * 128, (column + 1) * 128),
                jnp.concatenate([first, second], axis=0).astype(jnp.bfloat16),
            )

        for r in range(R):
            for k in range(2):
                for b in range(XB):
                    place(r, k, b, cell(r, b, 2 * k), cell(r, b, 2 * k + 1))
                for c in range(XB // 2):
                    one, two = cell(r, 2 * c, 4 + k), cell(r, 2 * c + 1, 4 + k)
                    place(
                        r, k, XB + c,
                        jnp.where(low, one, roll_half(two)),
                        jnp.where(low, roll_half(one), two),
                    )
        return carry

    lax.fori_loop(0, pairs // 4, step, 0)


def own_kernel(live_ref, next_ref, last_ref, before_ref, after_ref, a1_ref, out_ref, own_ref):
    own_ref[:16] = last_ref[:16]
    own_ref[16:20] = next_ref[12:16]
    own_ref[20:28] = last_ref[16:]
    own_ref[28:] = next_ref[22:]

    def fetch(i):
        return jnp.concatenate([own_ref[i], before_ref[i], after_ref[i]], axis=0)

    def one_slot(slot, carry):
        def put(r, rows, lanes, value):
            out_ref[slot, r, rows, lanes] = value

        stage_x(slot, 20, fetch, a1_ref, put, 0)
        return carry

    lax.fori_loop(0, live_ref[0], one_slot, 0)


def blur_own(live, cells, a1):
    vmem = pl.BlockSpec(memory_space=pltpu.VMEM)
    return pl.pallas_call(
        own_kernel,
        out_shape=jax.ShapeDtypeStruct((NEED, R, Y * XO, LANES), jnp.bfloat16),
        in_specs=[pl.BlockSpec(memory_space=pltpu.SMEM)] + [vmem] * 5,
        out_specs=vmem,
        scratch_shapes=[pltpu.VMEM((30, 80, NARROW), jnp.bfloat16)],
        compiler_params=pltpu.CompilerParams(vmem_limit_bytes=OWN_LIMIT),
        cost_estimate=pl.CostEstimate(flops=60000000000, bytes_accessed=2_000_000, transcendentals=0),
    )(live, *cells, a1)


def blur_kernel(
    live_ref, left_ref, left_ends, right_ref, right_ends, own_ref, a1_ref, a2_ref, a2b_ref, mask_ref, bz_ref,
    weights_ref, slot_ref, out_ref, line_x, line_y, band_y,
):
    out_ref[...] = jnp.zeros_like(out_ref)
    low_y = lax.broadcasted_iota(jnp.int32, (TOP * XO, NARROW), 1) < 64
    low_b = lax.broadcasted_iota(jnp.int32, ((Y - TOP) * XO, NARROW), 1) < 64
    side = HALF * XO

    def one_slot(slot, carry):
        def put(r, rows, lanes, value):
            line_x[r, rows, lanes] = value

        for cells, ends, offset in ((left_ref, left_ends, 0), (right_ref, right_ends, 8)):

            def fetch(i):
                return jnp.concatenate([cells[i], ends[i]], axis=0)

            stage_x(slot, 16, fetch, a1_ref, put, offset)

        def pair(q, carry):
            made = []
            for h in range(2):
                r = 2 * q + h
                top = a2_ref[slot * R + r]
                for o in range(XO):
                    band_y[h, o * TOP : (o + 1) * TOP, :] = top * mask_ref[o : o + 1, :]
                band_y[h, TOP * XO :, :] = a2b_ref[slot * R + r]
                lines = jnp.concatenate([line_x[r, :side], own_ref[slot, r], line_x[r, side:]], axis=0)
                made.append(jnp.dot(band_y[h], lines, preferred_element_type=jnp.float32))
            lanes = pl.multiple_of(q * 384, 128)
            tail = pl.ds(lanes + 256, 128)
            for first, count, start, low in ((0, TOP * XO, 0, low_y), (TOP * XO, (Y - TOP) * XO, TOP * X, low_b)):

                def cell(h, column):
                    return made[h][first : first + count, column * 128 : (column + 1) * 128]

                def rows(b):
                    return slice(start + b * count, start + (b + 1) * count)

                for b in range(XB):
                    for h in range(2):
                        line_y[rows(b), pl.ds(lanes + h * 128, 128)] = cell(h, b).astype(jnp.bfloat16)
                for c in range(XB // 2):
                    one, two = cell(0, XB + c), cell(1, XB + c)
                    line_y[rows(2 * c), tail] = jnp.where(low, one, roll_half(two)).astype(jnp.bfloat16)
                    line_y[rows(2 * c + 1), tail] = jnp.where(low, roll_half(one), two).astype(jnp.bfloat16)
            return carry

        lax.fori_loop(0, R // 2, pair, 0)

        done = jnp.dot(line_y[...], bz_ref[slot], preferred_element_type=jnp.float32)
        for low, high, made in ((0, TOP, done[:1280]), (TOP, Y, done[1280:])):
            weight = jnp.zeros((X, high - low, Z), jnp.float32)
            for j in range(2):
                here = slot_ref[j, :, low:high, :] == slot
                weight = weight + jnp.where(here, weights_ref[j, :, low:high, :].astype(jnp.float32), 0.0)
            out_ref[:, low:high, :] += weight * made.reshape(X, high - low, Z)
        return carry

    lax.fori_loop(0, live_ref[0], one_slot, 0)


def blur(live, cells, bands, weights, cell_slot):
    a1, a2, a2b, bz = bands
    inside, sides = cells
    own = blur_own(live, inside, a1)
    vmem = pl.BlockSpec(memory_space=pltpu.VMEM)
    mask = same_lane()
    return pl.pallas_call(
        blur_kernel,
        out_shape=jax.ShapeDtypeStruct((X, Y, Z), jnp.float32),
        in_specs=[pl.BlockSpec(memory_space=pltpu.SMEM)] + [vmem] * 12,
        out_specs=vmem,
        scratch_shapes=[
            pltpu.VMEM((R, 2 * HALF * XO, LANES), jnp.bfloat16),
            pltpu.VMEM((1600, 1536), jnp.bfloat16),
            pltpu.VMEM((2, Y * XO, EXT * XO), jnp.bfloat16),
        ],
        compiler_params=pltpu.CompilerParams(vmem_limit_bytes=BLUR_LIMIT),
    )(live, *sides, own, a1, a2, a2b, mask, bz, weights, cell_slot)


def doubled(rows, axis, bit):
    count = lax.axis_size(axis)
    other = lax.ppermute(rows, axis, [(i, i ^ bit) for i in range(count)])
    upper = (lax.axis_index(axis) & bit) != 0
    return jnp.concatenate(
        [jnp.where(upper, other, rows), jnp.where(upper, rows, other)], axis=0
    )


def both_ways(to_next, to_last, axis):
    count = lax.axis_size(axis)
    ends = count - 1
    after = lax.ppermute(to_last, axis, [((i + 1) % count, i) for i in range(ends)])
    before = lax.ppermute(to_next, axis, [(i, (i + 1) % count) for i in range(ends)])
    return before, after


def lane_part():
    return lax.broadcasted_iota(jnp.int32, (1, NARROW), 1) // HALF


def ends_kernel(reflect_ref, shallower_ref, deeper_ref):
    part = lane_part()
    for g in range(Y // 8):
        rows = [reflect_ref[:, 8 * g + k, :] for k in range(8)]
        for ref, first in ((deeper_ref, Z - HALF), (shallower_ref, 0)):
            packed = []
            for s in range(2):
                value = None
                for k in range(4):
                    shift = (k * HALF - first) % NARROW
                    turned = rows[2 * k + s]
                    turned = pltpu.roll(turned, shift, 1) if shift else turned
                    value = turned if value is None else jnp.where(part == k, turned, value)
                packed.append(value)
            ref[g] = jnp.concatenate(packed, axis=0).astype(jnp.bfloat16)


def depth_ends(reflect):
    vmem = pl.BlockSpec(memory_space=pltpu.VMEM)
    shapes = [(5, 80, NARROW), (5, 80, NARROW)]
    return pl.pallas_call(
        ends_kernel,
        out_shape=[jax.ShapeDtypeStruct(shape, jnp.bfloat16) for shape in shapes],
        in_specs=[vmem],
        out_specs=[vmem] * 2,
        compiler_params=pltpu.CompilerParams(vmem_limit_bytes=SMALL_LIMIT),
    )(reflect)


def cut_kernel(reflect_ref, after_ref, own_ref, next_ref, last_ref):
    for pair in range(Y // 2):
        two = [reflect_ref[:, 2 * pair + k, :] for k in range(2)]
        own_ref[pair] = jnp.concatenate(two, axis=0).astype(jnp.bfloat16)
        next_ref[pair] = jnp.concatenate([v[X - HALF :] for v in two], axis=0).astype(jnp.bfloat16)
        last_ref[pair] = jnp.concatenate([v[:HALF] for v in two], axis=0).astype(jnp.bfloat16)


def cut(reflect, after):
    shapes = [(20, 80, Z), (20, 64, Z), (20, 64, Z)]
    vmem = pl.BlockSpec(memory_space=pltpu.VMEM)
    return pl.pallas_call(
        cut_kernel,
        out_shape=[jax.ShapeDtypeStruct(shape, jnp.bfloat16) for shape in shapes],
        in_specs=[vmem, pl.BlockSpec(memory_space=pl.ANY)],
        out_specs=[vmem] * 3,
        compiler_params=pltpu.CompilerParams(vmem_limit_bytes=SMALL_LIMIT),
        cost_estimate=pl.CostEstimate(flops=8_000_000_000, bytes_accessed=2_000_000, transcendentals=0),
    )(reflect, after)


def tail_kernel(
    left_ref, right_ref, cells_ref, main_next, main_last, next_ref, last_ref, across_next, across_last
):
    part = lane_part()
    across_next[:16] = cells_ref[4:]
    across_last[:16] = cells_ref[:16]
    next_ref[:20] = main_next[...]
    last_ref[:20] = main_last[...]
    for g in range(5):
        left = left_ref[g].astype(jnp.float32)
        right = right_ref[g].astype(jnp.float32)
        for a in range(2):
            value = left if a == 0 else pltpu.roll(left, 64, 1)
            for k, (source, at) in enumerate(((right, 2 * a), (left, 2 * a + 1), (right, 2 * a + 1)), 1):
                shift = ((k - at) * HALF) % NARROW
                turned = pltpu.roll(source, shift, 1) if shift else source
                value = jnp.where(part == k, turned, value)
            tail = value.astype(jnp.bfloat16)
            if g > 0:
                across_next[16 + 2 * g + a - 2] = tail
            if g < 4:
                across_last[16 + 2 * g + a] = tail
            next_ref[20 + 2 * g + a] = jnp.concatenate(
                [value[X - HALF : X], value[2 * X - HALF :]], axis=0
            ).astype(jnp.bfloat16)
            last_ref[20 + 2 * g + a] = jnp.concatenate(
                [value[:HALF], value[X : X + HALF]], axis=0
            ).astype(jnp.bfloat16)


def unpack_tail(left, right, own, main_next, main_last):
    shapes = [(30, 64), (30, 64), (24, 80), (24, 80)]
    vmem = pl.BlockSpec(memory_space=pltpu.VMEM)
    return pl.pallas_call(
        tail_kernel,
        out_shape=[jax.ShapeDtypeStruct(shape + (NARROW,), jnp.bfloat16) for shape in shapes],
        in_specs=[vmem] * 5,
        out_specs=[vmem] * 4,
        compiler_params=pltpu.CompilerParams(vmem_limit_bytes=SMALL_LIMIT),
    )(left, right, own, main_next, main_last)


def join_kernel(before_ref, after_ref, rows_ref, left_ref, right_ref, next_ref, last_ref):
    for ref, to, at, count in (
        (next_ref, 0, 4, 16),
        (next_ref, 16, 22, 8),
        (last_ref, 0, 0, 16),
        (last_ref, 16, 20, 8),
    ):
        ref[to : to + count, 0:64, :] = before_ref[at : at + count]
        ref[to : to + count, 64:128, :] = after_ref[at : at + count]


def join(before, after, rows, left, right):
    vmem = pl.BlockSpec(memory_space=pltpu.VMEM)
    return pl.pallas_call(
        join_kernel,
        out_shape=[jax.ShapeDtypeStruct((24, 128, NARROW), jnp.bfloat16)] * 2,
        in_specs=[vmem] * 2 + [pl.BlockSpec(memory_space=pl.ANY)] * 3,
        out_specs=[vmem] * 2,
        compiler_params=pltpu.CompilerParams(vmem_limit_bytes=SMALL_LIMIT),
    )(before, after, rows, left, right)


def exchange(reflect, factors):
    shallower, deeper = depth_ends(reflect)
    above, below = both_ways(deeper, shallower, "gz")
    rows = doubled(factors, "xl", 1)
    own, to_next, to_last = cut(reflect, shallower)
    rows = doubled(rows, "xl", 2)
    to_next, to_last, across_next, across_last = unpack_tail(above, below, own, to_next, to_last)
    before, after = both_ways(to_next, to_last, "il")
    left, right = both_ways(across_next, across_last, "xl")
    to_next, to_last = join(before, after, rows, left, right)
    left_ends, right_ends = both_ways(to_next, to_last, "xl")
    rows = doubled(rows, "xl", 4)
    return ((across_next, across_last, before, after), (left, left_ends, right, right_ends)), rows


def per_device(reflect, weights, cell_slot, factors, reader_list):
    listed = reader_list.reshape(NEED)
    live_count = jnp.sum((listed >= 0).astype(jnp.int32))
    cells, rows = exchange(reflect, factors)
    bands = make_bands(listed, rows)
    return blur(live_count.reshape(1), cells, bands, weights, cell_slot)


def solution(mesh):
    in_specs = (
        P("il", "xl", "gz"),
        P(None, "il", "xl", "gz"),
        P(None, "il", "xl", "gz"),
        P(("il", "xl", "gz"), None),
        P("il", "xl", "gz", None),
    )
    out_specs = P("il", "xl", "gz")
    return jax.shard_map(
        per_device, mesh=mesh, in_specs=in_specs, out_specs=out_specs, check_vma=False
    )
```

```python
import jax
import jax.numpy as jnp
import numpy as np
from jax import lax
from jax.experimental import pallas as pl
from jax.experimental.pallas import tpu as pltpu
from jax.sharding import PartitionSpec as P

K = 64
R = 8
CP_DEV = 4
NEED = 3
HALF = 32
X, Y, Z = 40, 40, 128
XO = 4
XB = X // XO
LANES = XB * 192
SMALL_LIMIT = 10 * 1024 * 1024
OWN_LIMIT = 24 * 1024 * 1024
BLUR_LIMIT = 22 * 1024 * 1024
EXT = 104
ROWS = 2 * EXT
NARROW = 128
TOP = 32


def same_lane():
    return jnp.asarray(np.arange(EXT * XO)[None, :] % XO == np.arange(XO)[:, None], jnp.bfloat16)


def tap_maps():
    reverse = np.zeros((128, 128), np.float32)
    repeat = np.zeros((128, 256), np.float32)
    for t in range(K):
        reverse[t, -t % 128] = 1
        repeat[t, XO * t : XO * (t + 1)] = 1
    return jnp.asarray(np.concatenate([reverse, repeat], axis=1), jnp.bfloat16)


def bands_kernel(list_ref, table_ref, map_ref, a1_ref, a2_ref, a2b_ref, bz_ref, table, taps, long):
    for tile in range(12):
        table[tile] = table_ref[:, tile * 128 : (tile + 1) * 128].astype(jnp.float32)
    lane = lax.broadcasted_iota(jnp.int32, (1, 128), 1)
    for slot in range(NEED):
        listed = jnp.maximum(list_ref[slot], 0)
        key = (listed // (CP_DEV * 8)) % 8 * CP_DEV + listed % CP_DEV
        for r in range(R):
            for axis in range(3):
                tile, half = divmod(3 * r + axis, 2)
                piece = table[tile, pl.ds(key, 1), :]
                if half:
                    piece = pltpu.roll(piece, 64, 1)
                at = axis * NEED * R + slot * R + r
                taps[at : at + 1, :] = jnp.where(lane < K, piece, 0.0)
    mapped = jnp.dot(
        taps[...].astype(jnp.bfloat16), map_ref[...], preferred_element_type=jnp.float32
    )
    for tile in range(3):
        long[tile] = mapped[:, tile * 128 : (tile + 1) * 128]

    row8 = lax.broadcasted_iota(jnp.int32, (8, 128), 0)
    lane8 = lax.broadcasted_iota(jnp.int32, (8, 128), 1)
    low = row8 < 4

    def between(first, last):
        return (lane8 >= first) & (lane8 < last)

    parts = (
        (96, low & between(0, 40), None),
        (8, ~low & between(40, 80), None),
        (80, low & between(80, 112), None),
        (112, ~low & between(112, 128), ~low & between(0, 16)),
        (72, None, low & between(16, 48)),
        (104, None, ~low & between(48, 80)),
    )
    row_z = lax.broadcasted_iota(jnp.int32, (128, 128), 0)
    lane_z = lax.broadcasted_iota(jnp.int32, (128, 128), 1)
    inside = lane_z <= row_z
    row_y = lax.broadcasted_iota(jnp.int32, (TOP, 128), 0)
    lane_y = lax.broadcasted_iota(jnp.int32, (TOP, 128), 1)
    after = lane_y >= XO * row_y
    after8 = lane8 >= XO * row8

    def one_term(i, carry):
        slot = i // R
        r = i % R
        row = jnp.broadcast_to(taps[pl.ds(i, 1), :], (8, 128))
        base = pltpu.roll(row, 0, 1, stride=1, stride_axis=0)
        base = jnp.where(low, base, pltpu.roll(base, 124, 1))
        for b in range(0, XB, 2):
            ends = ([], [])
            for c in (b, b + 1):
                first = second = jnp.zeros((8, 128), jnp.float32)
                for shift, here, there in parts:
                    turned = pltpu.roll(base, (XO * c + shift) % 128, 1) if (XO * c + shift) % 128 else base
                    first = first if here is None else jnp.where(here, turned, first)
                    second = second if there is None else jnp.where(there, turned, second)
                ends[0].append(first)
                ends[1].append(second)
            rows = pl.ds(pl.multiple_of(r * (XB * 8) + b * 8, 16), 16)
            a1_ref[slot, rows, 0:128] = jnp.concatenate(ends[0], axis=0).astype(jnp.bfloat16)
            a1_ref[slot, rows, 128:ROWS] = jnp.concatenate(ends[1], axis=0)[:, : ROWS - 128].astype(jnp.bfloat16)
        halves = [
            pltpu.roll(
                jnp.broadcast_to(long[k, pl.ds(NEED * R + i, 1), :], (TOP, 128)),
                0, 1, stride=XO, stride_axis=0,
            )
            for k in (1, 2)
        ]
        zero = jnp.zeros((TOP, 128), jnp.float32)
        tiles = [
            jnp.where(after, halves[0], 0.0),
            jnp.where(after, halves[1], halves[0]),
            jnp.where(after, 0.0, halves[1]),
            zero,
        ]
        for k in range(4):
            width = min(128, EXT * XO - 128 * k)
            a2_ref[i, :, 128 * k : 128 * k + width] = tiles[k][:, :width].astype(jnp.bfloat16)
        ends = [
            jnp.zeros((8, 128), jnp.float32),
            jnp.where(after8, halves[0][:8], 0.0),
            jnp.where(after8, halves[1][:8], halves[0][:8]),
            jnp.where(after8, 0.0, halves[1][:8]),
        ]
        for k in range(4):
            width = min(128, EXT * XO - 128 * k)
            for o in range(0, XO, 2):
                two = jnp.concatenate(
                    [jnp.where(lane8 % XO == c, ends[k], 0.0) for c in (o, o + 1)], axis=0
                )
                a2b_ref[i, 8 * o : 8 * o + 16, 128 * k : 128 * k + width] = two[:, :width].astype(jnp.bfloat16)
        row = jnp.broadcast_to(long[0, pl.ds(2 * NEED * R + i, 1), :], (128, 128))
        turned = pltpu.roll(row, 0, 1, stride=1, stride_axis=0)
        first = jnp.where(inside, turned, 0.0).astype(jnp.bfloat16)
        second = jnp.where(inside, 0.0, turned).astype(jnp.bfloat16)
        start = (r // 2) * (2 * (Z + 2 * HALF))
        own = pl.multiple_of(start + (r % 2) * Z, 128)
        bz_ref[slot, pl.ds(own, 96), :] = first[32:]
        bz_ref[slot, pl.ds(own + 96, 32), :] = second[:32]
        ends = pl.multiple_of(start + 2 * Z + (r % 2) * 2 * HALF, 64)
        bz_ref[slot, pl.ds(ends, 32), :] = first[:32]
        bz_ref[slot, pl.ds(ends + 32, 32), :] = second[32:64]
        return carry

    lax.fori_loop(0, NEED * R, one_term, 0, unroll=4)


def make_bands(listed, table):
    shapes = [
        (NEED, R * XB * 8, ROWS),
        (NEED * R, TOP, EXT * XO),
        (NEED * R, XO * (Y - TOP), EXT * XO),
        (NEED, R * (Z + 2 * HALF), Z),
    ]
    vmem = pl.BlockSpec(memory_space=pltpu.VMEM)
    return pl.pallas_call(
        bands_kernel,
        out_shape=[jax.ShapeDtypeStruct(shape, jnp.bfloat16) for shape in shapes],
        in_specs=[pl.BlockSpec(memory_space=pltpu.SMEM), vmem, vmem],
        out_specs=[vmem] * 4,
        scratch_shapes=[
            pltpu.VMEM((12, 32, 128), jnp.float32),
            pltpu.VMEM((3 * NEED * R, 128), jnp.float32),
            pltpu.VMEM((3, 3 * NEED * R, 128), jnp.float32),
        ],
        compiler_params=pltpu.CompilerParams(vmem_limit_bytes=14 * 1024 * 1024),
        cost_estimate=pl.CostEstimate(flops=8000000000, bytes_accessed=2_000_000, transcendentals=0),
    )(listed, table, tap_maps())


def roll_half(value):
    return pltpu.roll(value, 64, 1)


def stage_x(slot, pairs, fetch, a1_ref, put, offset):
    low = lax.broadcasted_iota(jnp.int32, (8, NARROW), 1) < 64

    def step(i, carry):
        g = 2 * i
        rhs = jnp.concatenate(
            [fetch(4 * i + k) for k in range(4)] + [fetch(pairs + g + k) for k in range(2)],
            axis=1,
        )
        made = jnp.dot(a1_ref[slot], rhs, preferred_element_type=jnp.float32)
        base = pl.multiple_of((offset + g) * 16, 32)

        def cell(r, b, k):
            row = (r * XB + b) * 8
            return made[row : row + 8, k * 128 : (k + 1) * 128]

        def place(r, k, column, first, second):
            put(
                r,
                pl.ds(base + k * 16, 16),
                slice(column * 128, (column + 1) * 128),
                jnp.concatenate([first, second], axis=0).astype(jnp.bfloat16),
            )

        for r in range(R):
            for k in range(2):
                for b in range(XB):
                    place(r, k, b, cell(r, b, 2 * k), cell(r, b, 2 * k + 1))
                for c in range(XB // 2):
                    one, two = cell(r, 2 * c, 4 + k), cell(r, 2 * c + 1, 4 + k)
                    place(
                        r, k, XB + c,
                        jnp.where(low, one, roll_half(two)),
                        jnp.where(low, roll_half(one), two),
                    )
        return carry

    lax.fori_loop(0, pairs // 4, step, 0)


def own_kernel(live_ref, next_ref, last_ref, before_ref, after_ref, a1_ref, out_ref, own_ref):
    own_ref[:16] = last_ref[:16]
    own_ref[16:20] = next_ref[12:16]
    own_ref[20:28] = last_ref[16:]
    own_ref[28:] = next_ref[22:]

    def fetch(i):
        return jnp.concatenate([own_ref[i], before_ref[i], after_ref[i]], axis=0)

    def one_slot(slot, carry):
        def put(r, rows, lanes, value):
            out_ref[slot, r, rows, lanes] = value

        stage_x(slot, 20, fetch, a1_ref, put, 0)
        return carry

    lax.fori_loop(0, live_ref[0], one_slot, 0)


def blur_own(live, cells, a1):
    vmem = pl.BlockSpec(memory_space=pltpu.VMEM)
    return pl.pallas_call(
        own_kernel,
        out_shape=jax.ShapeDtypeStruct((NEED, R, Y * XO, LANES), jnp.bfloat16),
        in_specs=[pl.BlockSpec(memory_space=pltpu.SMEM)] + [vmem] * 5,
        out_specs=vmem,
        scratch_shapes=[pltpu.VMEM((30, 80, NARROW), jnp.bfloat16)],
        compiler_params=pltpu.CompilerParams(vmem_limit_bytes=OWN_LIMIT),
        cost_estimate=pl.CostEstimate(flops=60000000000, bytes_accessed=2_000_000, transcendentals=0),
    )(live, *cells, a1)


def blur_kernel(
    live_ref, left_ref, left_ends, right_ref, right_ends, own_ref, a1_ref, a2_ref, a2b_ref, mask_ref, bz_ref,
    weights_ref, slot_ref, out_ref, line_x, line_y, band_y,
):
    out_ref[...] = jnp.zeros_like(out_ref)
    low_y = lax.broadcasted_iota(jnp.int32, (TOP * XO, NARROW), 1) < 64
    low_b = lax.broadcasted_iota(jnp.int32, ((Y - TOP) * XO, NARROW), 1) < 64
    side = HALF * XO

    def one_slot(slot, carry):
        def put(r, rows, lanes, value):
            line_x[r, rows, lanes] = value

        for cells, ends, offset in ((left_ref, left_ends, 0), (right_ref, right_ends, 8)):

            def fetch(i):
                return jnp.concatenate([cells[i], ends[i]], axis=0)

            stage_x(slot, 16, fetch, a1_ref, put, offset)

        def pair(q, carry):
            made = []
            for h in range(2):
                r = 2 * q + h
                top = a2_ref[slot * R + r]
                for o in range(XO):
                    band_y[h, o * TOP : (o + 1) * TOP, :] = top * mask_ref[o : o + 1, :]
                band_y[h, TOP * XO :, :] = a2b_ref[slot * R + r]
                lines = jnp.concatenate([line_x[r, :side], own_ref[slot, r], line_x[r, side:]], axis=0)
                made.append(jnp.dot(band_y[h], lines, preferred_element_type=jnp.float32))
            lanes = pl.multiple_of(q * 384, 128)
            tail = pl.ds(lanes + 256, 128)
            for first, count, start, low in ((0, TOP * XO, 0, low_y), (TOP * XO, (Y - TOP) * XO, TOP * X, low_b)):

                def cell(h, column):
                    return made[h][first : first + count, column * 128 : (column + 1) * 128]

                def rows(b):
                    return slice(start + b * count, start + (b + 1) * count)

                for b in range(XB):
                    for h in range(2):
                        line_y[rows(b), pl.ds(lanes + h * 128, 128)] = cell(h, b).astype(jnp.bfloat16)
                for c in range(XB // 2):
                    one, two = cell(0, XB + c), cell(1, XB + c)
                    line_y[rows(2 * c), tail] = jnp.where(low, one, roll_half(two)).astype(jnp.bfloat16)
                    line_y[rows(2 * c + 1), tail] = jnp.where(low, roll_half(one), two).astype(jnp.bfloat16)
            return carry

        lax.fori_loop(0, R // 2, pair, 0)

        done = jnp.dot(line_y[...], bz_ref[slot], preferred_element_type=jnp.float32)
        for low, high, made in ((0, TOP, done[:1280]), (TOP, Y, done[1280:])):
            weight = jnp.zeros((X, high - low, Z), jnp.float32)
            for j in range(2):
                here = slot_ref[j, :, low:high, :] == slot
                weight = weight + jnp.where(here, weights_ref[j, :, low:high, :].astype(jnp.float32), 0.0)
            out_ref[:, low:high, :] += weight * made.reshape(X, high - low, Z)
        return carry

    lax.fori_loop(0, live_ref[0], one_slot, 0)


def blur(live, cells, bands, weights, cell_slot):
    a1, a2, a2b, bz = bands
    inside, sides = cells
    own = blur_own(live, inside, a1)
    vmem = pl.BlockSpec(memory_space=pltpu.VMEM)
    mask = same_lane()
    return pl.pallas_call(
        blur_kernel,
        out_shape=jax.ShapeDtypeStruct((X, Y, Z), jnp.float32),
        in_specs=[pl.BlockSpec(memory_space=pltpu.SMEM)] + [vmem] * 12,
        out_specs=vmem,
        scratch_shapes=[
            pltpu.VMEM((R, 2 * HALF * XO, LANES), jnp.bfloat16),
            pltpu.VMEM((1600, 1536), jnp.bfloat16),
            pltpu.VMEM((2, Y * XO, EXT * XO), jnp.bfloat16),
        ],
        compiler_params=pltpu.CompilerParams(vmem_limit_bytes=BLUR_LIMIT),
    )(live, *sides, own, a1, a2, a2b, mask, bz, weights, cell_slot)


def doubled(rows, axis, bit):
    count = lax.axis_size(axis)
    other = lax.ppermute(rows, axis, [(i, i ^ bit) for i in range(count)])
    upper = (lax.axis_index(axis) & bit) != 0
    return jnp.concatenate(
        [jnp.where(upper, other, rows), jnp.where(upper, rows, other)], axis=0
    )


def both_ways(to_next, to_last, axis):
    count = lax.axis_size(axis)
    ends = count - 1
    after = lax.ppermute(to_last, axis, [((i + 1) % count, i) for i in range(ends)])
    before = lax.ppermute(to_next, axis, [(i, (i + 1) % count) for i in range(ends)])
    return before, after


def lane_part():
    return lax.broadcasted_iota(jnp.int32, (1, NARROW), 1) // HALF


def ends_kernel(reflect_ref, shallower_ref, deeper_ref):
    part = lane_part()
    for g in range(Y // 8):
        rows = [reflect_ref[:, 8 * g + k, :] for k in range(8)]
        for ref, first in ((deeper_ref, Z - HALF), (shallower_ref, 0)):
            packed = []
            for s in range(2):
                value = None
                for k in range(4):
                    shift = (k * HALF - first) % NARROW
                    turned = rows[2 * k + s]
                    turned = pltpu.roll(turned, shift, 1) if shift else turned
                    value = turned if value is None else jnp.where(part == k, turned, value)
                packed.append(value)
            ref[g] = jnp.concatenate(packed, axis=0).astype(jnp.bfloat16)


def depth_ends(reflect):
    vmem = pl.BlockSpec(memory_space=pltpu.VMEM)
    shapes = [(5, 80, NARROW), (5, 80, NARROW)]
    return pl.pallas_call(
        ends_kernel,
        out_shape=[jax.ShapeDtypeStruct(shape, jnp.bfloat16) for shape in shapes],
        in_specs=[vmem],
        out_specs=[vmem] * 2,
        compiler_params=pltpu.CompilerParams(vmem_limit_bytes=SMALL_LIMIT),
    )(reflect)


def cut_kernel(reflect_ref, after_ref, own_ref, next_ref, last_ref):
    for pair in range(Y // 2):
        two = [reflect_ref[:, 2 * pair + k, :] for k in range(2)]
        own_ref[pair] = jnp.concatenate(two, axis=0).astype(jnp.bfloat16)
        next_ref[pair] = jnp.concatenate([v[X - HALF :] for v in two], axis=0).astype(jnp.bfloat16)
        last_ref[pair] = jnp.concatenate([v[:HALF] for v in two], axis=0).astype(jnp.bfloat16)


def cut(reflect, after):
    shapes = [(20, 80, Z), (20, 64, Z), (20, 64, Z)]
    vmem = pl.BlockSpec(memory_space=pltpu.VMEM)
    return pl.pallas_call(
        cut_kernel,
        out_shape=[jax.ShapeDtypeStruct(shape, jnp.bfloat16) for shape in shapes],
        in_specs=[vmem, pl.BlockSpec(memory_space=pl.ANY)],
        out_specs=[vmem] * 3,
        compiler_params=pltpu.CompilerParams(vmem_limit_bytes=SMALL_LIMIT),
        cost_estimate=pl.CostEstimate(flops=8_000_000_000, bytes_accessed=2_000_000, transcendentals=0),
    )(reflect, after)


def tail_kernel(
    left_ref, right_ref, cells_ref, main_next, main_last, next_ref, last_ref, across_next, across_last
):
    part = lane_part()
    across_next[:16] = cells_ref[4:]
    across_last[:16] = cells_ref[:16]
    next_ref[:20] = main_next[...]
    last_ref[:20] = main_last[...]
    for g in range(5):
        left = left_ref[g].astype(jnp.float32)
        right = right_ref[g].astype(jnp.float32)
        for a in range(2):
            value = left if a == 0 else pltpu.roll(left, 64, 1)
            for k, (source, at) in enumerate(((right, 2 * a), (left, 2 * a + 1), (right, 2 * a + 1)), 1):
                shift = ((k - at) * HALF) % NARROW
                turned = pltpu.roll(source, shift, 1) if shift else source
                value = jnp.where(part == k, turned, value)
            tail = value.astype(jnp.bfloat16)
            if g > 0:
                across_next[16 + 2 * g + a - 2] = tail
            if g < 4:
                across_last[16 + 2 * g + a] = tail
            next_ref[20 + 2 * g + a] = jnp.concatenate(
                [value[X - HALF : X], value[2 * X - HALF :]], axis=0
            ).astype(jnp.bfloat16)
            last_ref[20 + 2 * g + a] = jnp.concatenate(
                [value[:HALF], value[X : X + HALF]], axis=0
            ).astype(jnp.bfloat16)


def unpack_tail(left, right, own, main_next, main_last):
    shapes = [(30, 64), (30, 64), (24, 80), (24, 80)]
    vmem = pl.BlockSpec(memory_space=pltpu.VMEM)
    return pl.pallas_call(
        tail_kernel,
        out_shape=[jax.ShapeDtypeStruct(shape + (NARROW,), jnp.bfloat16) for shape in shapes],
        in_specs=[vmem] * 5,
        out_specs=[vmem] * 4,
        compiler_params=pltpu.CompilerParams(vmem_limit_bytes=SMALL_LIMIT),
    )(left, right, own, main_next, main_last)


def join_kernel(before_ref, after_ref, rows_ref, left_ref, right_ref, next_ref, last_ref):
    for ref, to, at, count in (
        (next_ref, 0, 4, 16),
        (next_ref, 16, 22, 8),
        (last_ref, 0, 0, 16),
        (last_ref, 16, 20, 8),
    ):
        ref[to : to + count, 0:64, :] = before_ref[at : at + count]
        ref[to : to + count, 64:128, :] = after_ref[at : at + count]


def join(before, after, rows, left, right):
    vmem = pl.BlockSpec(memory_space=pltpu.VMEM)
    return pl.pallas_call(
        join_kernel,
        out_shape=[jax.ShapeDtypeStruct((24, 128, NARROW), jnp.bfloat16)] * 2,
        in_specs=[vmem] * 2 + [pl.BlockSpec(memory_space=pl.ANY)] * 3,
        out_specs=[vmem] * 2,
        compiler_params=pltpu.CompilerParams(vmem_limit_bytes=SMALL_LIMIT),
    )(before, after, rows, left, right)


def exchange(reflect, factors):
    shallower, deeper = depth_ends(reflect)
    above, below = both_ways(deeper, shallower, "gz")
    rows = doubled(factors, "xl", 1)
    own, to_next, to_last = cut(reflect, shallower)
    rows = doubled(rows, "xl", 2)
    to_next, to_last, across_next, across_last = unpack_tail(above, below, own, to_next, to_last)
    before, after = both_ways(to_next, to_last, "il")
    left, right = both_ways(across_next, across_last, "xl")
    to_next, to_last = join(before, after, rows, left, left)
    left_ends, right_ends = both_ways(to_next, to_last, "xl")
    rows = doubled(rows, "xl", 4)
    return ((across_next, across_last, before, after), (left, left_ends, right, right_ends)), rows


def per_device(reflect, weights, cell_slot, factors, reader_list):
    listed = reader_list.reshape(NEED)
    live_count = jnp.sum((listed >= 0).astype(jnp.int32))
    cells, rows = exchange(reflect, factors)
    bands = make_bands(listed, rows)
    return blur(live_count.reshape(1), cells, bands, weights, cell_slot)


def solution(mesh):
    in_specs = (
        P("il", "xl", "gz"),
        P(None, "il", "xl", "gz"),
        P(None, "il", "xl", "gz"),
        P(("il", "xl", "gz"), None),
        P("il", "xl", "gz", None),
    )
    out_specs = P("il", "xl", "gz")
    return jax.shard_map(
        per_device, mesh=mesh, in_specs=in_specs, out_specs=out_specs, check_vma=False
    )
```
